32 devices in a mesh: row: 2 (over y), col: 16 (over z, x, core).
Axes of the slice: x: 2, y: 2, z: 4, core: 2. Of those that a mesh axis runs over, the one named last changes fastest.
Arguments:
- blocks: bfloat16 [64, 27, 128, 128], P(('row', 'col')), as said below
- columns: int32 [64, 27], P(('row', 'col')), may hold values from 0 to 63, as said below
- counts: int32 [64], P(('row', 'col')), may hold values from 1 to 27
Outputs:
- square: bfloat16 [64, 27, 128, 128], P(('row', 'col'))
- traces: float32 [2], replicated
The draws below stay inside these ranges and needn't reach their ends.
Inputs may be any that keep to these rules, and one draw needn't show every extreme that they name: `blocks`: exactly symmetric: slot w of block row i is the transpose of slot 26 - w of block row i + w - 13 whenever both rows lie in the window. The first counts[i] entries of row i are the block columns of row i's nonzero blocks in increasing order, each within 13 of i and inside the window; the diagonal block is always among them and the pattern is symmetric; later entries repeat the last one.
All inputs are finite; a program needn't handle non-finite values.
Results may differ from the reference program's by a relative error of at most 0.0012.
Values may be sent and summed in bfloat16 or wider, within the bound.
No kernel may reach another device: no remote copies, remote signals or barrier semaphores. Data moves between devices by JAX's collectives and lax.ppermute only.
A program may use at most 64 MiB of HBM per device.

```python
import math
import jax
import jax.numpy as jnp
from jax import lax

BS = 128
HALF = 13
ROWS_DEV = 2
NBLK = 64


def band_pattern(key):
    band_width = 2 * HALF + 1
    row_ids = jnp.arange(NBLK, dtype=jnp.int32)
    threshold = 72 + 24 * (row_ids * 8 // NBLK % 2)
    rolled = jax.random.randint(jax.random.fold_in(key, 7), (NBLK, HALF + 1), 0, 100)
    distances = jnp.arange(HALF + 1, dtype=jnp.int32)
    partner = row_ids[:, None] + distances[None, :]
    centre = NBLK // 2
    present_up = (rolled < threshold[:, None]) | (row_ids[:, None] == centre) | (partner == centre)
    present_up = present_up & (partner < NBLK)
    columns_list = []
    for slot_index in range(band_width):
        offset = slot_index - HALF
        if offset == 0:
            present = row_ids >= 0
        elif offset > 0:
            present = present_up[:, offset]
        else:
            present = jnp.roll(present_up[:, -offset], -offset) & (row_ids >= -offset)
        columns_list.append(present)
    present_all = jnp.stack(columns_list, axis=1)
    counted = jnp.sum(present_all.astype(jnp.int32), axis=1)
    slot_ids = jnp.arange(band_width, dtype=jnp.int32)
    scores = jnp.where(present_all, 0, band_width) + slot_ids[None, :]
    ordering = jnp.argsort(scores, axis=1).astype(jnp.int32)
    listed = row_ids[:, None] + ordering - HALF
    last_column = jnp.take_along_axis(listed, (counted - 1)[:, None], axis=1)
    columns = jnp.where(slot_ids[None, :] < counted[:, None], listed, last_column)
    return (columns.astype(jnp.int32), counted.astype(jnp.int32))


def draw_columns(key, part):
    return band_pattern(key)[0]


def draw_counts(key, part):
    return band_pattern(key)[1]


def draw_blocks(key, part):
    band_width = 2 * HALF + 1
    shape_all = (NBLK, band_width, BS, BS)
    values = jax.random.normal(jax.random.fold_in(key, 1), shape_all, jnp.float32)
    spread = 0.75
    row_ids = jnp.arange(NBLK, dtype=jnp.int32)
    ramp = 1.0 + spread * row_ids.astype(jnp.float32) / (NBLK - 1)
    factor = jnp.exp(jax.random.uniform(jax.random.fold_in(key, 2), (NBLK,), jnp.float32) * math.log(1.8)) * ramp
    base_scale = (8.0 * BS * band_width) ** (-0.5)
    slots_list = []
    for slot_index in range(band_width):
        offset = slot_index - HALF
        if offset == 0:
            diagonal = values[:, HALF]
            chosen = (diagonal + jnp.swapaxes(diagonal, 1, 2)) * 0.7071067811865476
        elif offset > 0:
            chosen = values[:, slot_index]
        else:
            chosen = jnp.swapaxes(jnp.roll(values[:, HALF - offset], -offset, axis=0), 1, 2)
        partner = jnp.clip(row_ids + offset, 0, NBLK - 1)
        pair_scale = base_scale * (factor * factor[partner])
        slots_list.append(chosen * pair_scale[:, None, None])
    return jnp.stack(slots_list, axis=1).astype(jnp.bfloat16)


def setup_inputs(seed: int = 0) -> dict:
    splits = jax.random.split(jax.random.key(seed), 4)
    blocks = draw_blocks(jax.random.fold_in(splits[3], 71), 0)
    columns = draw_columns(jax.random.fold_in(splits[3], 71), 0)
    counts = draw_counts(jax.random.fold_in(splits[3], 71), 0)
    return {"blocks": blocks, "columns": columns, "counts": counts}


def pattern_mask(columns, counts, first_row, half_band, band_width):
    slot_count = columns.shape[1]
    row_count = columns.shape[0]
    row_ids = first_row + jnp.arange(row_count, dtype=jnp.int32)
    offsets = columns - row_ids[:, None] + half_band
    in_list = jnp.arange(slot_count, dtype=jnp.int32)[None, :] < counts[:, None]
    targets = jnp.arange(band_width, dtype=jnp.int32)
    matches = (offsets[:, :, None] == targets[None, None, :]) & in_list[:, :, None]
    return jnp.sum(matches.astype(jnp.float32), axis=1)


def reference(blocks, columns, counts):
    total_rows = blocks.shape[0]
    band_width = blocks.shape[1]
    half_band = (band_width - 1) // 2
    block_size = blocks.shape[2]
    band_mask = pattern_mask(columns, counts, 0, half_band, band_width)
    density = blocks * band_mask.astype(blocks.dtype)[:, :, None, None]
    padded = jnp.pad(density, ((half_band, half_band), (0, 0), (0, 0), (0, 0)))
    first_rows = jnp.arange(0, total_rows, ROWS_DEV, dtype=jnp.int32)

    def one_panel(first_row):
        extended = lax.dynamic_slice_in_dim(padded, first_row, ROWS_DEV + 2 * half_band, 0).astype(jnp.float32)
        own_mask = lax.dynamic_slice_in_dim(band_mask, first_row, ROWS_DEV, 0)
        own_rows = extended[half_band:half_band + ROWS_DEV]
        results = []
        for offset in range(-half_band, half_band + 1):
            lower_slot = max(0, offset)
            upper_slot = min(band_width, band_width + offset)
            left_side = own_rows[:, lower_slot:upper_slot]
            right_side = extended[half_band + offset:half_band + offset + ROWS_DEV, lower_slot - offset:upper_slot - offset]
            results.append(jnp.einsum("lsxz,lsyz->lxy", left_side, right_side, precision=lax.Precision.HIGHEST))
        product = jnp.stack(results, axis=1) * own_mask[:, :, None, None]
        second = jnp.sum(jnp.trace(product[:, half_band], axis1=1, axis2=2))
        third = jnp.sum(own_rows * product)
        return product.astype(jnp.bfloat16), second, third

    square, second, third = lax.map(one_panel, first_rows)
    square = square.reshape(blocks.shape)
    traces = jnp.stack([jnp.sum(second), jnp.sum(third)]) / (total_rows * block_size)
    return square, traces
```

```python
import jax
import jax.numpy as jnp
from jax import lax
from jax.experimental import pallas as pl
from jax.experimental.pallas import tpu as pltpu
from jax.sharding import PartitionSpec as P

AXES = ("row", "col")
HALF = 13
BAND = 2 * HALF + 1
BS = 128
NEAR = HALF
FAR = 12
NCOL = NEAR + 1
NEAR_W, OWN_W, FAR_W = NCOL * BS, 4 * BS, FAR * BS
OWN_AT, FAR_AT = NEAR_W, NEAR_W + OWN_W
VMEM_LIMIT = 48 * 1024 * 1024

VM = pl.BlockSpec(memory_space=pltpu.VMEM)
SM = pl.BlockSpec(memory_space=pltpu.SMEM)


def params():
    return pltpu.CompilerParams(vmem_limit_bytes=VMEM_LIMIT)


def permute(value, target):
    devices = lax.axis_size(AXES)
    pairs = [(i, target(i)) for i in range(devices)]
    return lax.ppermute(value, AXES, [(i, j) for i, j in pairs if 0 <= j < devices])


def to_partner(value):
    return permute(value, lambda i: i ^ 1)


def to_side(value, distance):
    def target(i):
        chip, core = divmod(i, 2)
        return 2 * (chip + distance) if core else 2 * (chip - distance) + 1

    return permute(value, target)


def total(value):
    devices = lax.axis_size(AXES)
    if devices & (devices - 1):
        return lax.psum(value, AXES)
    step = 1
    while step < devices:
        value = value + permute(value, lambda i: i ^ step)
        step *= 2
    return value


def nn(a, b):
    return lax.dot_general(a, b, (((1,), (0,)), ((), ())), preferred_element_type=jnp.float32)


def nt(a, b):
    return lax.dot_general(a, b, (((1,), (1,)), ((), ())), preferred_element_type=jnp.float32)


def cut(i, n=1):
    return slice(i * BS, (i + n) * BS)


def own_kernel(meta, columns, counts, blocks, mine, other, mask, flags):
    core = meta[0]
    first_row = meta[1]
    for r in range(2):

        @pl.loop(0, BAND)
        def _(w):
            flags[r, w] = 0

        @pl.loop(0, counts[r])
        def _(n):
            flags[r, columns[r, n] - first_row - r + HALF] = 1

    for r in range(2):

        @pl.loop(0, BAND)
        def _(a):
            keep = flags[r, a]
            mask[r, a] = keep
            block = jnp.where(keep > 0, blocks[r, a], jnp.zeros((BS, BS), blocks.dtype))
            e = jnp.where(core > 0, 1 - r, r)
            w = jnp.where(core > 0, BAND - 1 - a, a)
            mine[e, w] = block
            other[1 - e, BAND - 1 - w] = block


def own_rows(meta, columns, counts, blocks):
    shape = jax.ShapeDtypeStruct(blocks.shape, blocks.dtype)
    return pl.pallas_call(
        own_kernel,
        out_shape=(shape, shape, jax.ShapeDtypeStruct((2, BAND), jnp.int32)),
        in_specs=[SM, SM, SM, VM],
        out_specs=(VM, VM, SM),
        scratch_shapes=[pltpu.SMEM((2, BAND), jnp.int32)],
        compiler_params=params(),
        name="own_rows",
    )(meta, columns, counts, blocks)


def fill_rows(mine, part, rows):
    zero = jnp.zeros((BS, BS), rows.dtype)

    def block(e, k):
        w = k - e + HALF
        if not 0 <= w < BAND:
            return zero
        return mine[e, w] if e < 2 else part[e - 2, w]

    for e in range(4):
        for t in range(1, NCOL + 1):
            rows[cut(e), cut(t - 1)] = block(e, -t)
        if rows.shape[1] > NEAR_W:
            for k in range(4):
                rows[cut(e), OWN_AT + k * BS : OWN_AT + (k + 1) * BS] = block(e, k)
            for u in range(1, FAR + 1):
                rows[cut(e), FAR_AT + (u - 1) * BS : FAR_AT + u * BS] = block(e, 3 + u)


def cross_start(t):
    return sum(11 - 2 * s for s in range(1, t))


def far_kernel(mine, part, cross, swapped, corner, partial, inner, sums, rows, upper, lower):
    fill_rows(mine, part, rows)
    zero = jnp.zeros((BS, BS), rows.dtype)

    def from_near(t, u):
        if t + u > 10:
            return zero
        if t == 5:
            return corner[0]
        return cross[cross_start(t) + 10 - t - u]

    def from_far(u, t):
        if t + u > 10:
            return zero
        return swapped[cross_start(u) + 10 - t - u]

    def tr(x):
        return jnp.transpose(x.astype(jnp.float32)).astype(x.dtype)

    for c in range(5):
        for g in range(c, 5 - c):
            for t in (2 * c + 1, 2 * c + 2):
                for u in (2 * g + 1, 2 * g + 2):
                    if t <= u or t + u > 10:
                        upper[cut(t - 1), cut(u - 1)] = from_near(t, u)
                    else:
                        upper[cut(t - 1), cut(u - 1)] = tr(from_far(u, t))
        for g in range(min(c, 5 - c)):
            for t in (2 * c + 1, 2 * c + 2):
                for u in (2 * g + 1, 2 * g + 2):
                    lower[cut(u - 1), cut(t - 1)] = from_far(u, t)

    third = jnp.zeros((1, 1), jnp.float32)
    own = rows[:, OWN_AT:FAR_AT]
    for c in range(NCOL // 2):
        near = rows[:, cut(2 * c, 2)]
        value = nn(own, near)
        if c < 3:
            value += nt(
                rows[:, FAR_AT + 2 * c * BS : FAR_AT + (10 - 2 * c) * BS],
                upper[cut(2 * c, 2), 2 * c * BS : (10 - 2 * c) * BS],
            )
        before = min(c, 5 - c)
        if before > 0:
            value += nn(
                rows[:, FAR_AT : FAR_AT + 2 * before * BS],
                lower[: 2 * before * BS, cut(2 * c, 2)],
            )
        partial[:, cut(2 * c, 2)] = value
        third += jnp.sum(near.astype(jnp.float32) * value, keepdims=True)
    third = 3.0 * third
    top = rows[: 2 * BS, OWN_AT:FAR_AT]
    third += jnp.sum(top.astype(jnp.float32) * nn(top, own), keepdims=True)
    inner[...] = nt(rows[: 2 * BS, :], rows[...])
    second = jnp.zeros((1, 1), jnp.float32)
    for e in range(2):
        for w in range(BAND):
            x = mine[e, w].astype(jnp.float32)
            second += jnp.sum(x * x, keepdims=True)
    sums[0:1, :] = jnp.broadcast_to(second, (1, BS))
    sums[1:2, :] = jnp.broadcast_to(third, (1, BS))


def far_part(mine, part, cross, swapped, corner):
    return pl.pallas_call(
        far_kernel,
        out_shape=(
            jax.ShapeDtypeStruct((4 * BS, NEAR_W), jnp.float32),
            jax.ShapeDtypeStruct((2 * BS, OWN_W), jnp.float32),
            jax.ShapeDtypeStruct((2, BS), jnp.float32),
        ),
        in_specs=[VM] * 5,
        out_specs=(VM,) * 3,
        scratch_shapes=[
            pltpu.VMEM((4 * BS, FAR_AT + FAR_W), jnp.bfloat16),
            pltpu.VMEM((10 * BS, 10 * BS), jnp.bfloat16),
            pltpu.VMEM((10 * BS, 10 * BS), jnp.bfloat16),
        ],
        compiler_params=params(),
        cost_estimate=pl.CostEstimate(flops=3 * 10**9, bytes_accessed=10**7, transcendentals=0),
        name="far_part",
    )(mine, part, cross, swapped, corner)


def near_start(t):
    first = 4 * ((t - 1) // 4) + 1
    return sum(14 - s for s in range(first, t))


def near_kernel(meta, mask, mine, part, d1, d2, d3, d4, partial, inner, out, away, rows, pairs):
    core = meta[0]
    fill_rows(mine, part, rows)
    zero = jnp.zeros((BS, BS), rows.dtype)
    packed = (d1, d2, d3, d4)

    def block(t, s):
        if s > NEAR:
            return zero
        return packed[(t - 1) // 4][near_start(t) + s - t]

    for t in range(1, NCOL + 1):
        for s in range(t, NCOL + 1):
            pairs[cut(t - 1), cut(s - 1)] = block(t, s)
        if t % 2 == 0:
            x = block(t - 1, t)
            x = jnp.transpose(x.astype(jnp.float32)).astype(x.dtype)
            pairs[cut(t - 1), cut(t - 2)] = x

    def put(e, w, value):
        r = jnp.where(core > 0, 1 - e, e)
        a = jnp.where(core > 0, BAND - 1 - w, w)
        keep = mask[r, a]
        out[r, a] = jnp.where(keep > 0, value, 0.0).astype(out.dtype)

    for e in range(2):
        for k in range(4):
            put(e, k - e + HALF, inner[cut(e), cut(k)])
    for c in range(NCOL // 2):
        value = partial[:, cut(2 * c, 2)]
        value += nt(rows[:, 2 * c * BS :], pairs[cut(2 * c, 2), 2 * c * BS :])
        if c > 0:
            value += nn(rows[:, : 2 * c * BS], pairs[: 2 * c * BS, cut(2 * c, 2)])
        for n in range(2):
            t = 2 * c + 1 + n
            for e in range(4):
                if e + t > HALF:
                    continue
                x = value[cut(e), cut(n)]
                if e < 2:
                    put(e, HALF - e - t, x)
                else:
                    away[(e - 2) * 11 + t - 1] = x.astype(away.dtype)


def near_part(meta, mask, mine, part, near, partial, inner):
    return pl.pallas_call(
        near_kernel,
        out_shape=(
            jax.ShapeDtypeStruct(mine.shape, mine.dtype),
            jax.ShapeDtypeStruct((21, BS, BS), mine.dtype),
        ),
        in_specs=[SM, SM] + [VM] * 8,
        out_specs=(VM, VM),
        scratch_shapes=[
            pltpu.VMEM((4 * BS, NEAR_W), jnp.bfloat16),
            pltpu.VMEM((NEAR_W, NEAR_W), jnp.bfloat16),
        ],
        compiler_params=params(),
        cost_estimate=pl.CostEstimate(flops=3 * 10**9, bytes_accessed=10**7, transcendentals=0),
        name="near_part",
    )(meta, mask, mine, part, *near, partial, inner)


def join_kernel(meta, mask, came, _, out, held, sems):
    core = meta[0]
    copies = []
    for e, count, base in ((0, 10, 11), (1, 11, 0)):
        r = jnp.where(core > 0, 1 - e, e)

        @pl.loop(0, count)
        def _(n):
            w = BAND - count + n
            a = jnp.where(core > 0, BAND - 1 - w, w)
            spot = jnp.where(core > 0, count - 1 - n, n)
            keep = mask[r, a]
            x = came[base + n]
            held[base + spot] = jnp.where(keep > 0, x, jnp.zeros_like(x))

        start = jnp.where(core > 0, 0, BAND - count)
        copy = pltpu.make_async_copy(
            held.at[pl.ds(base, count)], out.at[r, pl.ds(start, count)], sems.at[e]
        )
        copy.start()
        copies.append(copy)
    for copy in copies:
        copy.wait()


def join(meta, mask, came, out):
    anywhere = pl.BlockSpec(memory_space=pl.ANY)
    return pl.pallas_call(
        join_kernel,
        out_shape=jax.ShapeDtypeStruct(out.shape, out.dtype),
        in_specs=[SM, SM, VM, anywhere],
        out_specs=anywhere,
        scratch_shapes=[
            pltpu.VMEM(came.shape, came.dtype),
            pltpu.SemaphoreType.DMA((2,)),
        ],
        input_output_aliases={3: 0},
        compiler_params=params(),
        name="join",
    )(meta, mask, came, out)


def body(blocks, columns, counts):
    index = lax.axis_index(AXES)
    meta = jnp.stack([index % 2, index * 2]).astype(jnp.int32)
    mine, other, mask = own_rows(meta, columns, counts, blocks)
    part = to_partner(other)

    def row(e):
        return mine[e] if e < 2 else part[e - 2]

    cross = jnp.concatenate([row(e)[: 9 - 2 * e] for e in range(4)], axis=0)
    cross = to_side(cross, 1)
    corner = to_side(mine[0, :1], 2)
    near = []
    for distance in range(1, 5):
        runs = [(e, 4 * (distance - 1) + 1 + e) for e in range(4)]
        runs = [row(e)[HALF : BAND - t] for e, t in runs if t <= HALF]
        near.append(to_side(jnp.concatenate(runs, axis=0), distance))
    swapped = to_partner(cross)
    partial, inner, sums = far_part(mine, part, cross, swapped, corner)
    traces = total(sums[:, 0]) / (2 * BS * lax.axis_size(AXES))
    out, away = near_part(meta, mask, mine, part, near, partial, inner)
    square = join(meta, mask, to_partner(away), out)
    return square, traces


def solution(mesh):
    return jax.shard_map(
        body,
        mesh=mesh,
        in_specs=(P(AXES, None, None, None), P(AXES, None), P(AXES)),
        out_specs=(P(AXES, None, None, None), P()),
        check_vma=False,
    )
```

```python
import jax
import jax.numpy as jnp
from jax import lax
from jax.experimental import pallas as pl
from jax.experimental.pallas import tpu as pltpu
from jax.sharding import PartitionSpec as P

AXES = ("row", "col")
HALF = 13
BAND = 2 * HALF + 1
BS = 128
NEAR = HALF
FAR = 12
NCOL = NEAR + 1
NEAR_W, OWN_W, FAR_W = NCOL * BS, 4 * BS, FAR * BS
OWN_AT, FAR_AT = NEAR_W, NEAR_W + OWN_W
VMEM_LIMIT = 26 * 1024 * 1024

VM = pl.BlockSpec(memory_space=pltpu.VMEM)
SM = pl.BlockSpec(memory_space=pltpu.SMEM)
HB = pl.BlockSpec(memory_space=pl.ANY)


def params():
    return pltpu.CompilerParams(vmem_limit_bytes=VMEM_LIMIT)


def permute(value, target):
    devices = lax.axis_size(AXES)
    pairs = [(i, target(i)) for i in range(devices)]
    return lax.ppermute(value, AXES, [(i, j) for i, j in pairs if 0 <= j < devices])


def to_partner(value):
    return permute(value, lambda i: i ^ 1)


def to_side(value, distance, senders=lambda i: True):
    def target(i):
        chip, core = divmod(i, 2)
        if not senders(i):
            return -1
        return 2 * (chip + distance) if core else 2 * (chip - distance) + 1

    return permute(value, target)


def inner(i):
    return (i // 2 + i % 2) % 2 == 1


def add_over(value, *bits):
    first = bits[0]
    half = value + permute(value, lambda i: i ^ first)
    if len(bits) == 1:
        return half
    second = bits[1]
    other = permute(value, lambda i: i ^ second) + permute(value, lambda i: i ^ first ^ second)
    return half + other


def nn(a, b):
    return lax.dot_general(a, b, (((1,), (0,)), ((), ())), preferred_element_type=jnp.float32)


def nt(a, b):
    return lax.dot_general(a, b, (((1,), (1,)), ((), ())), preferred_element_type=jnp.float32)


def cut(i, n=1):
    return slice(i * BS, (i + n) * BS)


def own_kernel(meta, blocks, mine, other, mask):
    core = meta[2, 0]
    first_row = meta[2, 1]
    for r in range(2):
        for w in range(BAND):
            mask[r, w] = 0
    for r in range(2):

        @pl.loop(0, meta[2, 3 + r])
        def _(n):
            mask[r, meta[r, n] - first_row - r + HALF] = 1

    for r in range(2):
        e = jnp.where(core > 0, 1 - r, r)
        for a in range(BAND):
            x = jnp.where(mask[r, a] > 0, blocks[r, a], jnp.zeros((BS, BS), blocks.dtype))
            w = jnp.where(core > 0, BAND - 1 - a, a)
            mine[e, w] = x
            other[1 - e, BAND - 1 - w] = x


def own_rows(meta, blocks):
    shape = jax.ShapeDtypeStruct(blocks.shape, blocks.dtype)
    return pl.pallas_call(
        own_kernel,
        out_shape=(shape, shape, jax.ShapeDtypeStruct((2, BAND), jnp.int32)),
        in_specs=[SM, VM],
        out_specs=(VM, VM, SM),
        compiler_params=params(),
        name="own_rows",
    )(meta, blocks)


def low_slots(e):
    return [w for w in range(HALF, BAND - 1 - e) if e < 2 or not 5 <= w - HALF + 1 + e <= 8]


def first_kernel(mine, part, x1, z1, z2, direct):
    def put(out, at, e, slots):
        for w in slots:
            out[at] = mine[e, w] if e < 2 else part[e - 2, w]
            at += 1
        return at

    at1 = at2 = at3 = at4 = 0
    for e in range(4):
        at1 = put(x1, at1, e, range(9 - e))
        at2 = put(z1, at2, e, range(5 - e))
        at3 = put(z2, at3, e, range(HALF, BAND - 5 - e))
        at4 = put(direct, at4, 3 - e, range(HALF, HALF - 5 + e, -1))
    for e in range(4):
        at1 = put(x1, at1, e, low_slots(e))
        at2 = put(z1, at2, e, range(HALF, BAND - 1 - e))
    for e in range(4):
        at2 = put(z1, at2, e, range(HALF - 2 - e, HALF - e))
        at3 = put(z2, at3, e, range(HALF - 2 - e, HALF - e))


def first_packs(mine, part):
    return pl.pallas_call(
        first_kernel,
        out_shape=[jax.ShapeDtypeStruct((n, BS, BS), mine.dtype) for n in (68, 68, 38, 14)],
        in_specs=[VM] * 2,
        out_specs=[VM] * 4,
        compiler_params=params(),
        name="first_packs",
    )(mine, part)


def second_kernel(meta, x1, z1, corner, direct, _d4, _sums, cross, x2, d3):
    facing = meta[2, 2] > 0
    for n in range(30):
        cross[n] = x1[n]
    for n in range(14):
        cross[30 + n] = z1[n]
    cross[44] = corner[0]
    at, start = 0, 14
    for e in range(4):
        for w in low_slots(e):
            x2[at] = z1[start + w - HALF]
            at += 1
        start += 13 - e
    at, start = 0, 14
    for e in range(4):
        for n in range(5 - e):
            d3[at] = jnp.where(facing, z1[start + n], direct[at])
            at += 1
        start += 13 - e


def second_packs(meta, x1, z1, corner, direct, d4, sums):
    return pl.pallas_call(
        second_kernel,
        out_shape=[jax.ShapeDtypeStruct((n, BS, BS), x1.dtype) for n in (45, 38, 14)],
        in_specs=[SM] + [VM] * 6,
        out_specs=[VM] * 3,
        compiler_params=params(),
        name="second_packs",
    )(meta, x1, z1, corner, direct, d4, sums)


def turned(x):
    return jnp.transpose(x.astype(jnp.float32)).astype(x.dtype)


def fill_rows(mine, part, rows):
    zero = jnp.zeros((BS, BS), rows.dtype)

    def block(e, k):
        w = k - e + HALF
        if not 0 <= w < BAND:
            return zero
        return mine[e, w] if e < 2 else part[e - 2, w]

    for e in range(4):
        for t in range(1, NCOL + 1):
            rows[cut(e), cut(t - 1)] = block(e, -t)
        for k in range(4):
            rows[cut(e), OWN_AT + k * BS : OWN_AT + (k + 1) * BS] = block(e, k)
        for u in range(1, FAR + 1):
            rows[cut(e), FAR_AT + (u - 1) * BS : FAR_AT + u * BS] = block(e, 3 + u)


def near_start(t):
    first = 4 * ((t - 1) // 4) + 1
    return sum(14 - s for s in range(first, t))


def cross_start(t):
    return sum(10 - s for s in range(1, t))


def own_kernel_products(mine, part, own_sum, inner, near_rows, far_rows, sums, rows):
    fill_rows(mine, part, rows)
    near_rows[...] = rows[:, :NEAR_W]
    far_rows[...] = rows[:, FAR_AT : FAR_AT + 10 * BS]
    own = rows[:, OWN_AT:FAR_AT]
    third = jnp.zeros((1, 1), jnp.float32)
    for c in range(NCOL // 2):
        near = rows[:, cut(2 * c, 2)]
        value = nn(own, near)
        own_sum[:, cut(2 * c, 2)] = value
        third += jnp.sum(near.astype(jnp.float32) * value, keepdims=True)
    third = 3.0 * third
    top = rows[: 2 * BS, OWN_AT:FAR_AT]
    third += jnp.sum(top.astype(jnp.float32) * nn(top, own), keepdims=True)
    inner[...] = nt(rows[: 2 * BS, :], rows[...])
    second = jnp.zeros((1, 1), jnp.float32)
    for e in range(2):
        for w in range(BAND):
            x = mine[e, w].astype(jnp.float32)
            second += jnp.sum(x * x, keepdims=True)
    sums[0:1, :] = jnp.broadcast_to(second, (1, BS))
    sums[1:2, :] = jnp.broadcast_to(third, (1, BS))


def own_part(mine, part):
    return pl.pallas_call(
        own_kernel_products,
        out_shape=(
            jax.ShapeDtypeStruct((4 * BS, NEAR_W), jnp.float32),
            jax.ShapeDtypeStruct((2 * BS, OWN_W), jnp.float32),
            jax.ShapeDtypeStruct((4 * BS, NEAR_W), mine.dtype),
            jax.ShapeDtypeStruct((4 * BS, 10 * BS), mine.dtype),
            jax.ShapeDtypeStruct((2, BS), jnp.float32),
        ),
        in_specs=[VM] * 2,
        out_specs=(VM,) * 5,
        scratch_shapes=[pltpu.VMEM((4 * BS, FAR_AT + FAR_W), mine.dtype)],
        compiler_params=params(),
        cost_estimate=pl.CostEstimate(flops=2 * 10**9, bytes_accessed=10**6, transcendentals=0),
        name="own_part",
    )(mine, part)


def fill_cross(block, pairs):
    for c in range(5):
        for g in range(5 - c):
            for n in (2 * c + 1, 2 * c + 2):
                for m in (2 * g + 1, 2 * g + 2):
                    x = block(n, m) if n + m <= 10 else jnp.zeros((BS, BS), pairs.dtype)
                    pairs[cut(n - 1), cut(m - 1)] = x


def cross_kernel(near_rows, far_rows, own_sum, before, x1, z1, corner, first, sums, pairs):
    def block(t, u):
        at = cross_start(t) + 10 - t - u
        return x1[at] if t < 5 else z1[at - 30] if t < 9 else corner[0]

    fill_cross(block, pairs)
    third = jnp.zeros((1, 1), jnp.float32)
    for c in range(NCOL // 2):
        at = cut(2 * c, 2)
        if c < 5:
            width = (10 - 2 * c) * BS
            value = nt(far_rows[:, :width], pairs[at, :width])
            first[:, at] = own_sum[:, at] + value
            third += jnp.sum(near_rows[:, at].astype(jnp.float32) * value, keepdims=True)
        else:
            first[:, at] = own_sum[:, at]
    sums[0:1, :] = before[0:1, :]
    sums[1:2, :] = before[1:2, :] + 6.0 * third


def cross_part(near_rows, far_rows, own_sum, before, x1, z1, corner):
    return pl.pallas_call(
        cross_kernel,
        out_shape=(
            jax.ShapeDtypeStruct(own_sum.shape, jnp.float32),
            jax.ShapeDtypeStruct(before.shape, jnp.float32),
        ),
        in_specs=[VM] * 7,
        out_specs=(VM,) * 2,
        scratch_shapes=[pltpu.VMEM((10 * BS, 10 * BS), x1.dtype)],
        compiler_params=params(),
        cost_estimate=pl.CostEstimate(flops=10**9, bytes_accessed=10**6, transcendentals=0),
        name="cross_part",
    )(near_rows, far_rows, own_sum, before, x1, z1, corner)


LOW = 5


def mid_kernel(
    meta, near_rows, far_rows, before, swapped, z1, z2, d3, d4, partial, pairs, cross
):
    facing = meta[2, 2] > 0
    zero = jnp.zeros((BS, BS), pairs.dtype)
    fill_cross(lambda u, t: swapped[cross_start(u) + 10 - t - u], cross)

    def block(t, s):
        if s > NEAR:
            return zero
        if t == NEAR:
            return d4[0]
        if t > 8:
            return d3[near_start(t) + s - t]
        start = 14 + sum(13 - n for n in range(t - LOW))
        return jnp.where(facing, z1[start + s - t], z2[near_start(t) + s - t])

    for t in range(LOW, NCOL + 1):
        for s in range(t, NCOL + 1):
            pairs[cut(t - LOW), cut(s - LOW)] = block(t, s)
        if t % 2 == 0:
            pairs[cut(t - LOW), cut(t - 1 - LOW)] = turned(block(t - 1, t))
    low = (LOW - 1) * BS
    for c in range(NCOL // 2):
        at = 2 * c * BS
        value = before[:, at : at + 2 * BS]
        if c < 5:
            width = (10 - 2 * c) * BS
            value += nn(far_rows[:, :width], cross[:width, at : at + 2 * BS])
        if at >= low:
            value += nt(near_rows[:, at:], pairs[at - low : at - low + 2 * BS, at - low :])
        if at > low:
            value += nn(near_rows[:, low:at], pairs[: at - low, at - low : at - low + 2 * BS])
        partial[:, at : at + 2 * BS] = value


def mid_part(meta, near_rows, far_rows, before, swapped, z1, z2, d3, d4):
    return pl.pallas_call(
        mid_kernel,
        out_shape=jax.ShapeDtypeStruct(before.shape, before.dtype),
        in_specs=[SM] + [VM] * 8,
        out_specs=VM,
        scratch_shapes=[
            pltpu.VMEM((10 * BS, 10 * BS), near_rows.dtype),
            pltpu.VMEM((10 * BS, 10 * BS), near_rows.dtype),
        ],
        compiler_params=params(),
        cost_estimate=pl.CostEstimate(flops=3 * 10**9, bytes_accessed=10**6, transcendentals=0),
        name="mid_part",
    )(meta, near_rows, far_rows, before, swapped, z1, z2, d3, d4)


def fill_near(facing, x1, x2, z1, z2, pairs):
    def block(t, s):
        if t > 2 and 5 <= s <= 8:
            at = 2 * (s - LOW) + t - 3
            return turned(jnp.where(facing, z1[60 + at], z2[30 + at]))
        slots = low_slots(t - 1)
        at = sum(len(low_slots(n)) for n in range(t - 1)) + slots.index(HALF + s - t)
        return jnp.where(facing, x1[30 + at], x2[at])

    for t in range(1, 5):
        for s in range(1, NCOL + 1):
            if s > NEAR:
                x = jnp.zeros((BS, BS), pairs.dtype)
            else:
                x = turned(block(s, t)) if s < t else block(t, s)
            pairs[cut(t - 1), cut(s - 1)] = x


def near_products(half, near_rows, partial, pairs):
    rows = slice(2 * half * BS, (2 * half + 2) * BS)
    for c in range(NCOL // 2):
        value = partial[rows, cut(2 * c, 2)]
        if c < 2:
            value += nt(near_rows[rows, :], pairs[cut(2 * c, 2), :])
        else:
            value += nn(near_rows[rows, : 4 * BS], pairs[:, cut(2 * c, 2)])
        for n in range(2):
            t = 2 * c + 1 + n
            for e in range(2):
                if 2 * half + e + t <= HALF:
                    yield e, t, value[cut(e), cut(n)]


def away_kernel(meta, near_rows, partial, x1, x2, z1, z2, away, pairs):
    fill_near(meta[2, 2] > 0, x1, x2, z1, z2, pairs)
    for e, t, value in near_products(1, near_rows, partial, pairs):
        away[e * 11 + t - 1] = value.astype(away.dtype)


def away_part(meta, near_rows, partial, x1, x2, z1, z2):
    return pl.pallas_call(
        away_kernel,
        out_shape=jax.ShapeDtypeStruct((21, BS, BS), x1.dtype),
        in_specs=[SM] + [VM] * 6,
        out_specs=VM,
        scratch_shapes=[pltpu.VMEM((4 * BS, NEAR_W), x1.dtype)],
        compiler_params=params(),
        cost_estimate=pl.CostEstimate(flops=10**9, bytes_accessed=10**6, transcendentals=0),
        name="away_part",
    )(meta, near_rows, partial, x1, x2, z1, z2)


def near_kernel(meta, mask, near_rows, partial, inner, x1, x2, z1, z2, out, pairs):
    core = meta[2, 0]
    fill_near(meta[2, 2] > 0, x1, x2, z1, z2, pairs)

    def put(e, w, value):
        r = jnp.where(core > 0, 1 - e, e)
        a = jnp.where(core > 0, BAND - 1 - w, w)
        out[r, a] = jnp.where(mask[r, a] > 0, value, 0.0).astype(out.dtype)

    for e in range(2):
        for k in range(4):
            put(e, k - e + HALF, inner[cut(e), cut(k)])
    for e, t, value in near_products(0, near_rows, partial, pairs):
        put(e, HALF - e - t, value)


def near_part(meta, mask, near_rows, partial, inner, x1, x2, z1, z2):
    return pl.pallas_call(
        near_kernel,
        out_shape=jax.ShapeDtypeStruct((2, BAND, BS, BS), x1.dtype),
        in_specs=[SM] * 2 + [VM] * 7,
        out_specs=VM,
        scratch_shapes=[pltpu.VMEM((4 * BS, NEAR_W), x1.dtype)],
        compiler_params=params(),
        cost_estimate=pl.CostEstimate(flops=10**9, bytes_accessed=10**6, transcendentals=0),
        name="near_part",
    )(meta, mask, near_rows, partial, inner, x1, x2, z1, z2)


def join_kernel(meta, mask, came, _, out, held, sems):
    core = meta[2, 0]
    copies = []
    for e, count, base in ((0, 10, 11), (1, 11, 0)):
        r = jnp.where(core > 0, 1 - e, e)

        @pl.loop(0, count)
        def _(n):
            w = BAND - count + n
            a = jnp.where(core > 0, BAND - 1 - w, w)
            spot = jnp.where(core > 0, count - 1 - n, n)
            keep = mask[r, a]
            x = came[base + n]
            held[base + spot] = jnp.where(keep > 0, x, jnp.zeros_like(x))

        start = jnp.where(core > 0, 0, BAND - count)
        copy = pltpu.make_async_copy(
            held.at[pl.ds(base, count)], out.at[r, pl.ds(start, count)], sems.at[e]
        )
        copy.start()
        copies.append(copy)
    for copy in copies:
        copy.wait()


def join(meta, mask, came, out):
    anywhere = pl.BlockSpec(memory_space=pl.ANY)
    return pl.pallas_call(
        join_kernel,
        out_shape=jax.ShapeDtypeStruct(out.shape, out.dtype),
        in_specs=[SM, SM, VM, anywhere],
        out_specs=anywhere,
        scratch_shapes=[
            pltpu.VMEM(came.shape, came.dtype),
            pltpu.SemaphoreType.DMA((2,)),
        ],
        input_output_aliases={3: 0},
        compiler_params=params(),
        name="join",
    )(meta, mask, came, out)


def body(blocks, columns, counts):
    index = lax.axis_index(AXES)
    core, chip = index % 2, index // 2
    facing = (core + chip) % 2
    place = lax.broadcasted_iota(jnp.int32, (3, BAND), 1)
    scalars = jnp.where(place == 0, core, jnp.where(place == 1, index * 2, facing))
    table = jnp.pad(columns, ((0, 1), (0, 0))) + jnp.pad(counts[None], ((2, 0), (3, BAND - 5)))
    last = lax.broadcasted_iota(jnp.int32, (3, BAND), 0) == 2
    meta = jnp.where(last & (place < 3), scalars, table).astype(jnp.int32)
    mine, other, mask = own_rows(meta, blocks)
    part = to_partner(other)

    def outer(i):
        return not inner(i)

    x1, z1, z2, direct = first_packs(mine, part)
    x1 = to_side(x1, 1, inner)
    z1 = to_side(z1, 2, outer)
    corner = to_side(mine[0, :1], 3, inner)
    d4 = to_side(mine[0, HALF : HALF + 1], 4)
    z2 = to_side(z2, 2, inner)

    own_sum, inside, near_rows, far_rows, sums = own_part(mine, part)

    cross, x2, d3 = second_packs(meta, x1, z1, corner, direct, d4, sums)
    swapped = permute(cross, lambda i: i ^ 1 if inner(i) else -1)

    def across(i):
        chip, core = divmod(i, 2)
        return 2 * (chip + (1 if core else -1)) + core if inner(i) else -1

    x2 = permute(x2, across)

    def along(i):
        chip, core = divmod(i, 2)
        step = 1 if inner(i) else 3
        return 2 * (chip + (-step if core else step)) + core

    d3 = permute(d3, along)

    devices = lax.axis_size(AXES)
    first, sums = cross_part(near_rows, far_rows, own_sum, sums, x1, z1, corner)
    sums = sums[:, 0]
    steps = [1 << n for n in range(devices.bit_length() - 1)]
    steps = steps[:1] + steps[-1:] + steps[1:-1]
    for step in steps[:2] + steps[4:] + steps[2:3]:
        sums = add_over(sums, step)
    first, sums = lax.optimization_barrier((first, sums))
    partial = mid_part(meta, near_rows, far_rows, first, swapped, z1, z2, d3, d4)
    traces = add_over(sums, steps[3]) / (2 * BS * devices)
    away = away_part(meta, near_rows, partial, x1, x2, z1, z2)
    came = to_partner(away)
    out = near_part(meta, mask, near_rows, partial, inside, x1, x2, z1, z2)
    square = join(meta, mask, came, out)
    return square, traces


def solution(mesh):
    return jax.shard_map(
        body,
        mesh=mesh,
        in_specs=(P(AXES, None, None, None), P(AXES, None), P(AXES)),
        out_specs=(P(AXES, None, None, None), P()),
        check_vma=False,
    )
```

```python
import jax
import jax.numpy as jnp
from jax import lax
from jax.experimental import pallas as pl
from jax.experimental.pallas import tpu as pltpu
from jax.sharding import PartitionSpec as P

AXES = ("row", "col")
HALF = 13
BAND = 2 * HALF + 1
BS = 128
NEAR = HALF
FAR = 12
NCOL = NEAR + 1
NEAR_W, OWN_W, FAR_W = NCOL * BS, 4 * BS, FAR * BS
OWN_AT, FAR_AT = NEAR_W, NEAR_W + OWN_W
VMEM_LIMIT = 20 * 1024 * 1024

VM = pl.BlockSpec(memory_space=pltpu.VMEM)
SM = pl.BlockSpec(memory_space=pltpu.SMEM)
HB = pl.BlockSpec(memory_space=pl.ANY)


def params():
    return pltpu.CompilerParams(vmem_limit_bytes=VMEM_LIMIT)


def permute(value, target):
    devices = lax.axis_size(AXES)
    pairs = [(i, target(i)) for i in range(devices)]
    return lax.ppermute(value, AXES, [(i, j) for i, j in pairs if 0 <= j < devices])


def to_partner(value):
    return permute(value, lambda i: i ^ 1)


def to_side(value, distance, senders=lambda i: True):
    def target(i):
        chip, core = divmod(i, 2)
        if not senders(i):
            return -1
        return 2 * (chip + distance) if core else 2 * (chip - distance) + 1

    return permute(value, target)


def inner(i):
    return (i // 2 + i % 2) % 2 == 1


def all_sums(value):
    devices = lax.axis_size(AXES)
    steps = [1 << n for n in range(devices.bit_length() - 1)]
    for step in steps[:1] + steps[4:] + steps[1:4]:
        value = value + permute(value, lambda i: i ^ step)
    return value


def nn(a, b):
    return lax.dot_general(a, b, (((1,), (0,)), ((), ())), preferred_element_type=jnp.float32)


def nt(a, b):
    return lax.dot_general(a, b, (((1,), (1,)), ((), ())), preferred_element_type=jnp.float32)


def cut(i, n=1):
    return slice(i * BS, (i + n) * BS)


def my_core():
    return lax.rem(lax.axis_index("col"), 2)


def faces_pair():
    index = lax.axis_index("row") * lax.axis_size("col") + lax.axis_index("col")
    return lax.rem(lax.div(index, 2) + lax.rem(index, 2), 2) > 0


def own_kernel(table, blocks, mine, other, mask, flags):
    core = my_core()
    first_row = 2 * (lax.axis_index("row") * lax.axis_size("col") + lax.axis_index("col"))
    for r in range(2):
        for w in range(BAND):
            flags[r, w] = 0
    for r in range(2):

        @pl.loop(0, table[2, r])
        def _(n):
            flags[r, table[r, n] - first_row - r + HALF] = 1

    for r in range(2):
        e = jnp.where(core > 0, 1 - r, r)
        for a in range(BAND):
            keep = flags[r, a]
            mask[r, a] = jnp.full((1, BS), keep, jnp.int32)
            x = jnp.where(keep > 0, blocks[r, a], jnp.zeros((BS, BS), blocks.dtype))
            w = jnp.where(core > 0, BAND - 1 - a, a)
            mine[e, w] = x
            other[1 - e, BAND - 1 - w] = x


def own_rows(table, blocks):
    shape = jax.ShapeDtypeStruct(blocks.shape, blocks.dtype)
    return pl.pallas_call(
        own_kernel,
        out_shape=(shape, shape, jax.ShapeDtypeStruct((2, BAND, 1, BS), jnp.int32)),
        in_specs=[SM, VM],
        out_specs=(VM, VM, VM),
        scratch_shapes=[pltpu.SMEM((2, BAND), jnp.int32)],
        compiler_params=params(),
        name="own_rows",
    )(table, blocks)


def low_slots(e):
    return [w for w in range(HALF, BAND - 1 - e) if e < 2 or not 5 <= w - HALF + 1 + e <= 8]


def first_kernel(mine, part, x1, z1, z2, single):
    at = {}

    def put(out, e, slots):
        for w in slots:
            n = at.get(id(out), 0)
            out[n] = mine[e, w] if e < 2 else part[e - 2, w]
            at[id(out)] = n + 1

    for e in range(4):
        put(x1, e, range(9 - e))
    for e in range(4):
        put(z1, e, range(5 - e))
    for e in range(4):
        put(z2, e, range(HALF, BAND - 5 - e))
    for e in range(4):
        put(x1, e, low_slots(e))
    for e in range(4):
        put(z1, e, range(HALF, BAND - 1 - e))
    for e in range(4):
        put(z1, e, range(HALF - 2 - e, HALF - e))
        put(z2, e, range(HALF - 2 - e, HALF - e))
    single[0] = jnp.where(faces_pair(), mine[0, 0], part[1, HALF])


def first_packs(mine, part):
    return pl.pallas_call(
        first_kernel,
        out_shape=[jax.ShapeDtypeStruct((n, BS, BS), mine.dtype) for n in (68, 68, 38, 1)],
        in_specs=[VM] * 2,
        out_specs=[VM] * 4,
        compiler_params=params(),
        name="first_packs",
    )(mine, part)


def second_kernel(x1, z1, single, _, cross, x2, g, h):
    for n in range(30):
        cross[n] = x1[n]
    for n in range(14):
        cross[30 + n] = z1[n]
    cross[44] = single[0]
    at1 = at2 = at3 = 0
    start_x, start_z = 30, 14
    for e in range(4):
        for w in low_slots(e):
            x2[at1] = z1[start_z + w - HALF]
            at1 += 1
        for n in range(5 - e):
            g[at2] = z1[start_z + n]
            if n < 4 - e or e < 2:
                h[at2] = x1[start_x + n]
            else:
                h[at2] = turned(z1[60 + e - 2])
            at2 += 1
        start_x += len(low_slots(e))
        start_z += 13 - e
    h[at2] = z1[14]


def second_packs(x1, z1, single, sums):
    return pl.pallas_call(
        second_kernel,
        out_shape=[jax.ShapeDtypeStruct((n, BS, BS), x1.dtype) for n in (45, 38, 14, 15)],
        in_specs=[VM] * 4,
        out_specs=[VM] * 4,
        compiler_params=params(),
        name="second_packs",
    )(x1, z1, single, sums)


def turned(x):
    return jnp.transpose(x.astype(jnp.float32)).astype(x.dtype)


def fill_rows(mine, part, rows):
    zero = jnp.zeros((BS, BS), rows.dtype)

    def block(e, k):
        w = k - e + HALF
        if not 0 <= w < BAND:
            return zero
        return mine[e, w] if e < 2 else part[e - 2, w]

    for e in range(4):
        for t in range(1, NCOL + 1):
            rows[cut(e), cut(t - 1)] = block(e, -t)
        for k in range(4):
            rows[cut(e), OWN_AT + k * BS : OWN_AT + (k + 1) * BS] = block(e, k)
        for u in range(1, FAR + 1):
            rows[cut(e), FAR_AT + (u - 1) * BS : FAR_AT + u * BS] = block(e, 3 + u)


def fill_pairs(block, near, low, pairs):
    for t in near:
        for s in range(low, NCOL + 1):
            if s > NEAR:
                x = jnp.zeros((BS, BS), pairs.dtype)
            else:
                x = turned(block(s, t)) if s < t else block(t, s)
            pairs[cut(t - low), cut(s - low)] = x


def near_start(t):
    first = 4 * ((t - 1) // 4) + 1
    return sum(14 - s for s in range(first, t))


def cross_start(t):
    return sum(10 - s for s in range(1, t))


def own_kernel_products(mine, part, own_rows, inner, near_rows, far_rows, sums, rows):
    fill_rows(mine, part, rows)
    own_rows[...] = rows[:, OWN_AT:FAR_AT]
    near_rows[...] = rows[:, :NEAR_W]
    far_rows[...] = rows[:, FAR_AT : FAR_AT + 10 * BS]
    own = rows[:, OWN_AT:FAR_AT]
    third = jnp.zeros((1, 1), jnp.float32)
    for c in range(NCOL // 2):
        near = rows[:, cut(2 * c, 2)]
        value = nn(own, near)
        third += jnp.sum(near.astype(jnp.float32) * value, keepdims=True)
    third = 3.0 * third
    top = rows[: 2 * BS, OWN_AT:FAR_AT]
    third += jnp.sum(top.astype(jnp.float32) * nn(top, own), keepdims=True)
    inner[...] = nt(rows[: 2 * BS, :], rows[...])
    second = jnp.zeros((1, 1), jnp.float32)
    for e in range(2):
        for w in range(BAND):
            x = mine[e, w].astype(jnp.float32)
            second += jnp.sum(x * x, keepdims=True)
    sums[0:1, :] = jnp.broadcast_to(second, (1, BS))
    sums[1:2, :] = jnp.broadcast_to(third, (1, BS))


def own_part(mine, part):
    return pl.pallas_call(
        own_kernel_products,
        out_shape=(
            jax.ShapeDtypeStruct((4 * BS, OWN_W), mine.dtype),
            jax.ShapeDtypeStruct((2 * BS, OWN_W), jnp.float32),
            jax.ShapeDtypeStruct((4 * BS, NEAR_W), mine.dtype),
            jax.ShapeDtypeStruct((4 * BS, 10 * BS), mine.dtype),
            jax.ShapeDtypeStruct((2, BS), jnp.float32),
        ),
        in_specs=[VM] * 2,
        out_specs=(VM,) * 5,
        scratch_shapes=[pltpu.VMEM((4 * BS, FAR_AT + FAR_W), mine.dtype)],
        compiler_params=params(),
        cost_estimate=pl.CostEstimate(flops=2 * 10**9, bytes_accessed=10**6, transcendentals=0),
        name="own_part",
    )(mine, part)


def fill_cross(block, pairs):
    for c in range(5):
        for g in range(5 - c):
            for n in (2 * c + 1, 2 * c + 2):
                for m in (2 * g + 1, 2 * g + 2):
                    x = block(n, m) if n + m <= 10 else jnp.zeros((BS, BS), pairs.dtype)
                    pairs[cut(n - 1), cut(m - 1)] = x


def cross_kernel(near_rows, far_rows, before, x1, z1, single, first, sums, pairs):
    def block(t, u):
        at = cross_start(t) + 10 - t - u
        if t == 9:
            return jnp.where(faces_pair(), single[0], jnp.zeros((BS, BS), pairs.dtype))
        return x1[at] if t < 5 else z1[at - 30]

    fill_cross(block, pairs)
    third = jnp.zeros((1, 1), jnp.float32)
    for c in range(5):
        at = cut(2 * c, 2)
        width = (10 - 2 * c) * BS
        value = nt(far_rows[:, :width], pairs[at, :width])
        first[:, at] = value
        third += jnp.sum(near_rows[:, at].astype(jnp.float32) * value, keepdims=True)
    sums[0:1, :] = before[0:1, :]
    sums[1:2, :] = before[1:2, :] + 6.0 * third


def cross_part(near_rows, far_rows, before, x1, z1, single):
    return pl.pallas_call(
        cross_kernel,
        out_shape=(
            jax.ShapeDtypeStruct((4 * BS, 10 * BS), jnp.float32),
            jax.ShapeDtypeStruct(before.shape, jnp.float32),
        ),
        in_specs=[VM] * 6,
        out_specs=(VM,) * 2,
        scratch_shapes=[pltpu.VMEM((10 * BS, 10 * BS), x1.dtype)],
        compiler_params=params(),
        cost_estimate=pl.CostEstimate(flops=10**9, bytes_accessed=10**6, transcendentals=0),
        name="cross_part",
    )(near_rows, far_rows, before, x1, z1, single)


def mid_kernel(own, near_rows, far_rows, first, swapped, partial, cross):
    fill_cross(lambda u, t: swapped[cross_start(u) + 10 - t - u], cross)
    for c in range(NCOL // 2):
        at = cut(2 * c, 2)
        value = nn(own[...], near_rows[:, at])
        if c < 5:
            width = (10 - 2 * c) * BS
            value += first[:, at]
            value += nn(far_rows[:, :width], cross[:width, at])
        partial[:, at] = value


def mid_part(own, near_rows, far_rows, first, swapped):
    return pl.pallas_call(
        mid_kernel,
        out_shape=jax.ShapeDtypeStruct(near_rows.shape, jnp.float32),
        in_specs=[VM] * 5,
        out_specs=VM,
        scratch_shapes=[pltpu.VMEM((10 * BS, 10 * BS), near_rows.dtype)],
        compiler_params=params(),
        cost_estimate=pl.CostEstimate(flops=2 * 10**9, bytes_accessed=10**6, transcendentals=0),
        name="mid_part",
    )(own, near_rows, far_rows, first, swapped)


LOW, LAST = 5, 9


def fill_near(facing, x1, x2, z1, z2, g, h, single, pairs1, pairs2, pairs3):
    def block(t, s):
        if t == NEAR:
            return jnp.where(facing, h[14], single[0])
        if t >= LAST:
            at = near_start(t) + s - t
            return jnp.where(facing, h[at], g[at])
        if t >= LOW:
            start = 14 + sum(13 - n for n in range(t - LOW))
            return jnp.where(facing, z1[start + s - t], z2[near_start(t) + s - t])
        if t > 2 and LOW <= s < LAST:
            at = 2 * (s - LOW) + t - 3
            return turned(jnp.where(facing, z1[60 + at], z2[30 + at]))
        slots = low_slots(t - 1)
        at = sum(len(low_slots(n)) for n in range(t - 1)) + slots.index(HALF + s - t)
        return jnp.where(facing, x1[30 + at], x2[at])

    fill_pairs(block, range(1, LOW), 1, pairs1)
    fill_pairs(block, range(LOW, LAST), LOW, pairs2)
    fill_pairs(block, range(LAST, NEAR + 1), LAST, pairs3)
    pairs3[cut(NCOL - LAST), :] = jnp.zeros((BS, (NCOL + 1 - LAST) * BS), pairs3.dtype)


def near_products(half, near_rows, partial, pairs1, pairs2, pairs3):
    rows = slice(2 * half * BS, (2 * half + 2) * BS)
    two, three = (LOW - 1) * BS, (LAST - 1) * BS
    for c in range(NCOL // 2):
        at = 2 * c * BS
        to = at + 2 * BS
        value = partial[rows, at:to]
        if at < two:
            value += nt(near_rows[rows, :], pairs1[at:to, :])
        else:
            value += nn(near_rows[rows, :two], pairs1[:, at:to])
        if two <= at < three:
            value += nt(near_rows[rows, two:], pairs2[at - two : to - two, :])
        elif at >= three:
            value += nn(near_rows[rows, two:three], pairs2[:, at - two : to - two])
            value += nt(near_rows[rows, three:], pairs3[at - three : to - three, :])
        for n in range(2):
            t = 2 * c + 1 + n
            for e in range(2):
                if 2 * half + e + t <= HALF:
                    yield e, t, value[cut(e), cut(n)]


def away_kernel(near_rows, partial, x1, x2, z1, z2, g, h, single, away, pairs1, pairs2, pairs3):
    fill_near(faces_pair(), x1, x2, z1, z2, g, h, single, pairs1, pairs2, pairs3)
    for e, t, value in near_products(1, near_rows, partial, pairs1, pairs2, pairs3):
        away[e * 11 + t - 1] = value.astype(away.dtype)


def away_part(near_rows, partial, x1, x2, z1, z2, g, h, single):
    shapes = (21, BS, BS), (4 * BS, NEAR_W), (4 * BS, 10 * BS), (6 * BS, 6 * BS)
    return pl.pallas_call(
        away_kernel,
        out_shape=[jax.ShapeDtypeStruct(shape, x1.dtype) for shape in shapes],
        in_specs=[VM] * 9,
        out_specs=[VM] * 4,
        compiler_params=params(),
        cost_estimate=pl.CostEstimate(flops=2 * 10**9, bytes_accessed=10**6, transcendentals=0),
        name="away_part",
    )(near_rows, partial, x1, x2, z1, z2, g, h, single)


def near_kernel(mask, near_rows, partial, inner, pairs1, pairs2, pairs3, out):
    core = my_core()

    def put(e, w, value):
        r = jnp.where(core > 0, 1 - e, e)
        a = jnp.where(core > 0, BAND - 1 - w, w)
        out[r, a] = jnp.where(mask[r, a] > 0, value, 0.0).astype(out.dtype)

    for e in range(2):
        for k in range(4):
            put(e, k - e + HALF, inner[cut(e), cut(k)])
    for e, t, value in near_products(0, near_rows, partial, pairs1, pairs2, pairs3):
        put(e, HALF - e - t, value)


def near_part(mask, near_rows, partial, inner, *pairs):
    return pl.pallas_call(
        near_kernel,
        out_shape=jax.ShapeDtypeStruct((2, BAND, BS, BS), near_rows.dtype),
        in_specs=[VM] * 7,
        out_specs=VM,
        compiler_params=params(),
        cost_estimate=pl.CostEstimate(flops=10**9, bytes_accessed=10**6, transcendentals=0),
        name="near_part",
    )(mask, near_rows, partial, inner, *pairs)


def join_kernel(mask, came, _, out, held, sems):
    core = my_core()
    copies = []
    for e, count, base in ((0, 10, 11), (1, 11, 0)):
        r = jnp.where(core > 0, 1 - e, e)

        @pl.loop(0, count)
        def _(n):
            w = BAND - count + n
            a = jnp.where(core > 0, BAND - 1 - w, w)
            spot = jnp.where(core > 0, count - 1 - n, n)
            x = came[base + n]
            held[base + spot] = jnp.where(mask[r, a] > 0, x, jnp.zeros_like(x))

        start = jnp.where(core > 0, 0, BAND - count)
        copy = pltpu.make_async_copy(
            held.at[pl.ds(base, count)], out.at[r, pl.ds(start, count)], sems.at[e]
        )
        copy.start()
        copies.append(copy)
    for copy in copies:
        copy.wait()


def join(mask, came, out):
    anywhere = pl.BlockSpec(memory_space=pl.ANY)
    return pl.pallas_call(
        join_kernel,
        out_shape=jax.ShapeDtypeStruct(out.shape, out.dtype),
        in_specs=[VM, VM, anywhere],
        out_specs=anywhere,
        scratch_shapes=[
            pltpu.VMEM(came.shape, came.dtype),
            pltpu.SemaphoreType.DMA((2,)),
        ],
        input_output_aliases={2: 0},
        compiler_params=params(),
        name="join",
    )(mask, came, out)


def body(blocks, columns, counts):
    table = jnp.pad(columns, ((0, 1), (0, 0))) + jnp.pad(counts[None], ((2, 0), (0, BAND - 2)))
    mine, other, mask = own_rows(table, blocks)
    part = to_partner(other)

    def outer(i):
        return not inner(i)

    x1, z1, z2, single = first_packs(mine, part)
    x1 = to_side(x1, 1, inner)
    z1 = to_side(z1, 2, outer)

    def singles(i):
        chip, core = divmod(i, 2)
        if inner(i):
            return 2 * (chip + 3) if core else 2 * (chip - 3) + 1
        return 2 * (chip - 4) + 1 if core else 2 * (chip + 4)

    single = permute(single, singles)
    own, inside, near_rows, far_rows, sums = own_part(mine, part)

    cross, x2, g, h = second_packs(x1, z1, single, sums)
    swapped = permute(cross, lambda i: i ^ 1 if inner(i) else -1)

    def along(pair, senders):
        def target(i):
            chip, core = divmod(i, 2)
            return 2 * (chip + (pair if core else -pair)) + core if senders(i) else -1

        return target

    z2 = to_side(z2, 2, inner)
    x2 = permute(x2, along(1, inner))
    g = permute(g, along(-1, inner))
    h = permute(h, along(-2, inner))

    first, sums = cross_part(near_rows, far_rows, sums, x1, z1, single)
    sums, swapped = lax.optimization_barrier((sums[:, 0], swapped))
    sums = all_sums(sums)
    partial = mid_part(own, near_rows, far_rows, first, swapped)
    partial, sums = lax.optimization_barrier((partial, sums))
    traces = sums / (2 * BS * lax.axis_size(AXES))
    away, *pairs = away_part(near_rows, partial, x1, x2, z1, z2, g, h, single)
    came = to_partner(away)
    out = near_part(mask, near_rows, partial, inside, *pairs)
    square = join(mask, came, out)
    return square, traces


def solution(mesh):
    return jax.shard_map(
        body,
        mesh=mesh,
        in_specs=(P(AXES, None, None, None), P(AXES, None), P(AXES)),
        out_specs=(P(AXES, None, None, None), P()),
        check_vma=False,
    )
```

```python
import jax
import jax.numpy as jnp
from jax import lax
from jax.experimental import pallas as pl
from jax.experimental.pallas import tpu as pltpu
from jax.sharding import PartitionSpec as P

AXES = ("row", "col")
HALF = 13
BAND = 2 * HALF + 1
BS = 128
NEAR = HALF
FAR = 12
NCOL = NEAR + 1
NEAR_W, OWN_W, FAR_W = NCOL * BS, 4 * BS, FAR * BS
OWN_AT, FAR_AT = NEAR_W, NEAR_W + OWN_W
VMEM_LIMIT = 20 * 1024 * 1024

VM = pl.BlockSpec(memory_space=pltpu.VMEM)
SM = pl.BlockSpec(memory_space=pltpu.SMEM)
HB = pl.BlockSpec(memory_space=pl.ANY)


def params():
    return pltpu.CompilerParams(vmem_limit_bytes=VMEM_LIMIT)


def permute(value, target):
    devices = lax.axis_size(AXES)
    pairs = [(i, target(i)) for i in range(devices)]
    return lax.ppermute(value, AXES, [(i, j) for i, j in pairs if 0 <= j < devices])


def to_partner(value):
    return permute(value, lambda i: i ^ 1)


def to_side(value, distance, senders=lambda i: True):
    def target(i):
        chip, core = divmod(i, 2)
        if not senders(i):
            return -1
        return 2 * (chip + distance) if core else 2 * (chip - distance) + 1

    return permute(value, target)


def inner(i):
    return (i // 2 + i % 2) % 2 == 1


def sum_over(value, steps):
    for step in steps:
        value = value + permute(value, lambda i: i ^ step)
    return value


def nn(a, b):
    return lax.dot_general(a, b, (((1,), (0,)), ((), ())), preferred_element_type=jnp.float32)


def nt(a, b):
    return lax.dot_general(a, b, (((1,), (1,)), ((), ())), preferred_element_type=jnp.float32)


def cut(i, n=1):
    return slice(i * BS, (i + n) * BS)


def my_core():
    return lax.rem(lax.axis_index("col"), 2)


def faces_pair():
    index = lax.axis_index("row") * lax.axis_size("col") + lax.axis_index("col")
    return lax.rem(lax.div(index, 2) + lax.rem(index, 2), 2) > 0


def own_kernel(table, blocks, mine, other, mask, flags):
    core = my_core()
    first_row = 2 * (lax.axis_index("row") * lax.axis_size("col") + lax.axis_index("col"))
    for r in range(2):
        for w in range(BAND):
            flags[r, w] = 0
    for r in range(2):

        @pl.loop(0, table[2, r])
        def _(n):
            flags[r, table[r, n] - first_row - r + HALF] = 1

    for r in range(2):
        e = jnp.where(core > 0, 1 - r, r)
        for a in range(BAND):
            keep = flags[r, a]
            mask[r, a] = jnp.full((1, BS), keep, jnp.int32)
            x = jnp.where(keep > 0, blocks[r, a], jnp.zeros((BS, BS), blocks.dtype))
            w = jnp.where(core > 0, BAND - 1 - a, a)
            mine[e, w] = x
            other[1 - e, BAND - 1 - w] = x


def own_rows(table, blocks):
    shape = jax.ShapeDtypeStruct(blocks.shape, blocks.dtype)
    return pl.pallas_call(
        own_kernel,
        out_shape=(shape, shape, jax.ShapeDtypeStruct((2, BAND, 1, BS), jnp.int32)),
        in_specs=[SM, VM],
        out_specs=(VM, VM, VM),
        scratch_shapes=[pltpu.SMEM((2, BAND), jnp.int32)],
        compiler_params=params(),
        name="own_rows",
    )(table, blocks)


def low_slots(e):
    return [w for w in range(HALF, BAND - 1 - e) if e < 3 or not 5 <= w - HALF + 1 + e <= 8]


def first_kernel(mine, part, x1, z1, z2, single):
    at = {}

    def put(out, e, slots):
        for w in slots:
            n = at.get(id(out), 0)
            out[n] = mine[e, w] if e < 2 else part[e - 2, w]
            at[id(out)] = n + 1

    for e in range(4):
        put(x1, e, range(9 - e))
    for e in range(4):
        put(z1, e, range(5 - e))
    for e in range(4):
        put(z2, e, range(HALF, BAND - 5 - e))
    for e in range(4):
        put(x1, e, low_slots(e))
    for e in range(4):
        put(z1, e, range(HALF, BAND - 1 - e))
    for e in range(4):
        put(z1, e, range(HALF - 1 - e, HALF - e))
        put(z2, e, range(HALF - 1 - e, HALF - e))
    single[0] = jnp.where(faces_pair(), mine[0, 0], part[1, HALF])


def first_packs(mine, part):
    return pl.pallas_call(
        first_kernel,
        out_shape=[jax.ShapeDtypeStruct((n, BS, BS), mine.dtype) for n in (72, 64, 34, 1)],
        in_specs=[VM] * 2,
        out_specs=[VM] * 4,
        compiler_params=params(),
        name="first_packs",
    )(mine, part)


def second_kernel(x1, z1, _, x2, g, h):
    at1 = at2 = 0
    start_x, start_z = 30, 14
    for e in range(4):
        for w in low_slots(e):
            x2[at1] = z1[start_z + w - HALF]
            at1 += 1
        for n in range(5 - e):
            g[at2] = z1[start_z + n]
            h[at2] = x1[start_x + n] if n < 4 - e or e < 3 else turned(z1[60])
            at2 += 1
        start_x += len(low_slots(e))
        start_z += 13 - e
    h[at2] = z1[14]


def second_packs(x1, z1, sums):
    return pl.pallas_call(
        second_kernel,
        out_shape=[jax.ShapeDtypeStruct((n, BS, BS), x1.dtype) for n in (42, 14, 15)],
        in_specs=[VM] * 3,
        out_specs=[VM] * 3,
        compiler_params=params(),
        name="second_packs",
    )(x1, z1, sums)


def join_cross_kernel(x1, z1, single, _, cross):
    for n in range(30):
        cross[n] = x1[n]
    for n in range(14):
        cross[30 + n] = z1[n]
    cross[44] = single[0]


def join_cross(x1, z1, single, sums):
    return pl.pallas_call(
        join_cross_kernel,
        out_shape=jax.ShapeDtypeStruct((45, BS, BS), x1.dtype),
        in_specs=[VM] * 4,
        out_specs=VM,
        compiler_params=params(),
        name="join_cross",
    )(x1, z1, single, sums)


def turned(x):
    return jnp.transpose(x.astype(jnp.float32)).astype(x.dtype)


def fill_rows(mine, part, rows):
    zero = jnp.zeros((BS, BS), rows.dtype)

    def block(e, k):
        w = k - e + HALF
        if not 0 <= w < BAND:
            return zero
        return mine[e, w] if e < 2 else part[e - 2, w]

    for e in range(4):
        for t in range(1, NCOL + 1):
            rows[cut(e), cut(t - 1)] = block(e, -t)
        for k in range(4):
            rows[cut(e), OWN_AT + k * BS : OWN_AT + (k + 1) * BS] = block(e, k)
        for u in range(1, FAR + 1):
            rows[cut(e), FAR_AT + (u - 1) * BS : FAR_AT + u * BS] = block(e, 3 + u)


def fill_pairs(block, near, low, pairs):
    for t in near:
        for s in range(low, NCOL + 1):
            if s > NEAR:
                x = jnp.zeros((BS, BS), pairs.dtype)
            else:
                x = turned(block(s, t)) if s < t else block(t, s)
            pairs[cut(t - low), cut(s - low)] = x


def near_start(t):
    first = 4 * ((t - 1) // 4) + 1
    return sum(14 - s for s in range(first, t))


def cross_start(t):
    return sum(10 - s for s in range(1, t))


def own_kernel_products(mine, part, own_rows, inner, near_rows, far_rows, sums, rows):
    fill_rows(mine, part, rows)
    own_rows[...] = rows[:, OWN_AT:FAR_AT]
    near_rows[...] = rows[:, :NEAR_W]
    far_rows[...] = rows[:, FAR_AT : FAR_AT + 10 * BS]
    own = rows[:, OWN_AT:FAR_AT]
    third = jnp.zeros((1, 1), jnp.float32)
    for c in range(NCOL // 2):
        near = rows[:, cut(2 * c, 2)]
        value = nn(own, near)
        third += jnp.sum(near.astype(jnp.float32) * value, keepdims=True)
    third = 3.0 * third
    top = rows[: 2 * BS, OWN_AT:FAR_AT]
    third += jnp.sum(top.astype(jnp.float32) * nn(top, own), keepdims=True)
    inner[...] = nt(rows[: 2 * BS, :], rows[...])
    second = jnp.zeros((1, 1), jnp.float32)
    for e in range(2):
        for w in range(BAND):
            x = mine[e, w].astype(jnp.float32)
            second += jnp.sum(x * x, keepdims=True)
    sums[0:1, :] = jnp.broadcast_to(second, (1, BS))
    sums[1:2, :] = jnp.broadcast_to(third, (1, BS))


def own_part(mine, part):
    return pl.pallas_call(
        own_kernel_products,
        out_shape=(
            jax.ShapeDtypeStruct((4 * BS, OWN_W), mine.dtype),
            jax.ShapeDtypeStruct((2 * BS, OWN_W), jnp.float32),
            jax.ShapeDtypeStruct((4 * BS, NEAR_W), mine.dtype),
            jax.ShapeDtypeStruct((4 * BS, 10 * BS), mine.dtype),
            jax.ShapeDtypeStruct((2, BS), jnp.float32),
        ),
        in_specs=[VM] * 2,
        out_specs=(VM,) * 5,
        scratch_shapes=[pltpu.VMEM((4 * BS, FAR_AT + FAR_W), mine.dtype)],
        compiler_params=params(),
        cost_estimate=pl.CostEstimate(flops=2 * 10**9, bytes_accessed=10**6, transcendentals=0),
        name="own_part",
    )(mine, part)


def fill_cross(block, pairs):
    for c in range(5):
        for g in range(5 - c):
            for n in (2 * c + 1, 2 * c + 2):
                for m in (2 * g + 1, 2 * g + 2):
                    x = block(n, m) if n + m <= 10 else jnp.zeros((BS, BS), pairs.dtype)
                    pairs[cut(n - 1), cut(m - 1)] = x


def cross_kernel(near_rows, far_rows, before, x1, z1, single, first, sums, pairs):
    def block(t, u):
        at = cross_start(t) + 10 - t - u
        if t == 9:
            return jnp.where(faces_pair(), single[0], jnp.zeros((BS, BS), pairs.dtype))
        return x1[at] if t < 5 else z1[at - 30]

    fill_cross(block, pairs)
    third = jnp.zeros((1, 1), jnp.float32)
    for c in range(5):
        at = cut(2 * c, 2)
        width = (10 - 2 * c) * BS
        value = nt(far_rows[:, :width], pairs[at, :width])
        first[:, at] = value
        third += jnp.sum(near_rows[:, at].astype(jnp.float32) * value, keepdims=True)
    scale = 1.0 / (2 * BS * lax.axis_size(AXES))
    sums[0:1, :] = before[0:1, :] * scale
    sums[1:2, :] = (before[1:2, :] + 6.0 * third) * scale


def cross_part(near_rows, far_rows, before, x1, z1, single):
    return pl.pallas_call(
        cross_kernel,
        out_shape=(
            jax.ShapeDtypeStruct((4 * BS, 10 * BS), jnp.float32),
            jax.ShapeDtypeStruct(before.shape, jnp.float32),
        ),
        in_specs=[VM] * 6,
        out_specs=(VM,) * 2,
        scratch_shapes=[pltpu.VMEM((10 * BS, 10 * BS), x1.dtype)],
        compiler_params=params(),
        cost_estimate=pl.CostEstimate(flops=10**9, bytes_accessed=10**6, transcendentals=0),
        name="cross_part",
    )(near_rows, far_rows, before, x1, z1, single)


def mid_kernel(own, near_rows, far_rows, first, swapped, partial, cross):
    fill_cross(lambda u, t: swapped[cross_start(u) + 10 - t - u], cross)
    for c in range(NCOL // 2):
        at = cut(2 * c, 2)
        value = nn(own[...], near_rows[:, at])
        if c < 5:
            width = (10 - 2 * c) * BS
            value += first[:, at]
            value += nn(far_rows[:, :width], cross[:width, at])
        partial[:, at] = value


def mid_part(own, near_rows, far_rows, first, swapped):
    return pl.pallas_call(
        mid_kernel,
        out_shape=jax.ShapeDtypeStruct(near_rows.shape, jnp.float32),
        in_specs=[VM] * 5,
        out_specs=VM,
        scratch_shapes=[pltpu.VMEM((10 * BS, 10 * BS), near_rows.dtype)],
        compiler_params=params(),
        cost_estimate=pl.CostEstimate(flops=2 * 10**9, bytes_accessed=10**6, transcendentals=0),
        name="mid_part",
    )(own, near_rows, far_rows, first, swapped)


LOW, LAST = 5, 9


def fill_near(facing, x1, x2, z1, z2, g, h, single, pairs1, pairs2, pairs3):
    def block(t, s):
        if t == NEAR:
            return jnp.where(facing, h[14], single[0])
        if t >= LAST:
            at = near_start(t) + s - t
            return jnp.where(facing, h[at], g[at])
        if t >= LOW:
            start = 14 + sum(13 - n for n in range(t - LOW))
            return jnp.where(facing, z1[start + s - t], z2[near_start(t) + s - t])
        if t == 4 and LOW <= s < LAST:
            at = s - LOW
            return turned(jnp.where(facing, z1[60 + at], z2[30 + at]))
        slots = low_slots(t - 1)
        at = sum(len(low_slots(n)) for n in range(t - 1)) + slots.index(HALF + s - t)
        return jnp.where(facing, x1[30 + at], x2[at])

    fill_pairs(block, range(1, LOW), 1, pairs1)
    fill_pairs(block, range(LOW, LAST), LOW, pairs2)
    fill_pairs(block, range(LAST, NEAR + 1), LAST, pairs3)
    pairs3[cut(NCOL - LAST), :] = jnp.zeros((BS, (NCOL + 1 - LAST) * BS), pairs3.dtype)


def near_products(half, near_rows, partial, pairs1, pairs2, pairs3):
    rows = slice(2 * half * BS, (2 * half + 2) * BS)
    two, three = (LOW - 1) * BS, (LAST - 1) * BS
    for c in range(NCOL // 2):
        at = 2 * c * BS
        to = at + 2 * BS
        value = partial[rows, at:to]
        if at < two:
            value += nt(near_rows[rows, :], pairs1[at:to, :])
        else:
            value += nn(near_rows[rows, :two], pairs1[:, at:to])
        if two <= at < three:
            value += nt(near_rows[rows, two:], pairs2[at - two : to - two, :])
        elif at >= three:
            value += nn(near_rows[rows, two:three], pairs2[:, at - two : to - two])
            value += nt(near_rows[rows, three:], pairs3[at - three : to - three, :])
        for n in range(2):
            t = 2 * c + 1 + n
            for e in range(2):
                if 2 * half + e + t <= HALF:
                    yield e, t, value[cut(e), cut(n)]


def away_kernel(near_rows, partial, x1, x2, z1, z2, g, h, single, away, pairs1, pairs2, pairs3):
    fill_near(faces_pair(), x1, x2, z1, z2, g, h, single, pairs1, pairs2, pairs3)
    for e, t, value in near_products(1, near_rows, partial, pairs1, pairs2, pairs3):
        away[e * 11 + t - 1] = value.astype(away.dtype)


def away_part(near_rows, partial, x1, x2, z1, z2, g, h, single):
    shapes = (21, BS, BS), (4 * BS, NEAR_W), (4 * BS, 10 * BS), (6 * BS, 6 * BS)
    return pl.pallas_call(
        away_kernel,
        out_shape=[jax.ShapeDtypeStruct(shape, x1.dtype) for shape in shapes],
        in_specs=[VM] * 9,
        out_specs=[VM] * 4,
        compiler_params=params(),
        cost_estimate=pl.CostEstimate(flops=2 * 10**9, bytes_accessed=10**6, transcendentals=0),
        name="away_part",
    )(near_rows, partial, x1, x2, z1, z2, g, h, single)


def near_kernel(mask, near_rows, partial, inner, pairs1, pairs2, pairs3, out):
    core = my_core()

    def put(e, w, value):
        r = jnp.where(core > 0, 1 - e, e)
        a = jnp.where(core > 0, BAND - 1 - w, w)
        out[r, a] = jnp.where(mask[r, a] > 0, value, 0.0).astype(out.dtype)

    for e in range(2):
        for k in range(4):
            put(e, k - e + HALF, inner[cut(e), cut(k)])
    for e, t, value in near_products(0, near_rows, partial, pairs1, pairs2, pairs3):
        put(e, HALF - e - t, value)


def near_part(mask, near_rows, partial, inner, *pairs):
    return pl.pallas_call(
        near_kernel,
        out_shape=jax.ShapeDtypeStruct((2, BAND, BS, BS), near_rows.dtype),
        in_specs=[VM] * 7,
        out_specs=VM,
        compiler_params=params(),
        cost_estimate=pl.CostEstimate(flops=10**9, bytes_accessed=10**6, transcendentals=0),
        name="near_part",
    )(mask, near_rows, partial, inner, *pairs)


def join_kernel(mask, came, _, out, held, sems):
    core = my_core()
    copies = []
    for e, count, base in ((0, 10, 11), (1, 11, 0)):
        r = jnp.where(core > 0, 1 - e, e)

        @pl.loop(0, count)
        def _(n):
            w = BAND - count + n
            a = jnp.where(core > 0, BAND - 1 - w, w)
            spot = jnp.where(core > 0, count - 1 - n, n)
            x = came[base + n]
            held[base + spot] = jnp.where(mask[r, a] > 0, x, jnp.zeros_like(x))

        start = jnp.where(core > 0, 0, BAND - count)
        copy = pltpu.make_async_copy(
            held.at[pl.ds(base, count)], out.at[r, pl.ds(start, count)], sems.at[e]
        )
        copy.start()
        copies.append(copy)
    for copy in copies:
        copy.wait()


def join(mask, came, out):
    anywhere = pl.BlockSpec(memory_space=pl.ANY)
    return pl.pallas_call(
        join_kernel,
        out_shape=jax.ShapeDtypeStruct(out.shape, out.dtype),
        in_specs=[VM, VM, anywhere],
        out_specs=anywhere,
        scratch_shapes=[
            pltpu.VMEM(came.shape, came.dtype),
            pltpu.SemaphoreType.DMA((2,)),
        ],
        input_output_aliases={2: 0},
        compiler_params=params(),
        name="join",
    )(mask, came, out)


def body(blocks, columns, counts):
    table = jnp.pad(columns, ((0, 1), (0, 0))) + jnp.pad(counts[None], ((2, 0), (0, BAND - 2)))
    mine, other, mask = own_rows(table, blocks)
    part = to_partner(other)

    def outer(i):
        return not inner(i)

    x1, z1, z2, single = first_packs(mine, part)
    x1 = to_side(x1, 1, inner)
    z1 = to_side(z1, 2, outer)

    def singles(i):
        chip, core = divmod(i, 2)
        if inner(i):
            return 2 * (chip + 3) if core else 2 * (chip - 3) + 1
        return 2 * (chip - 4) + 1 if core else 2 * (chip + 4)

    single = permute(single, singles)
    own, inside, near_rows, far_rows, sums = own_part(mine, part)

    x2, g, h = second_packs(x1, z1, sums)
    swapped = permute(join_cross(x1, z1, single, g), lambda i: i ^ 1 if inner(i) else -1)

    def along(pair, senders):
        def target(i):
            chip, core = divmod(i, 2)
            return 2 * (chip + (pair if core else -pair)) + core if senders(i) else -1

        return target

    z2 = to_side(z2, 2, inner)
    x2 = permute(x2, along(1, inner))
    g = permute(g, along(-1, inner))
    h = permute(h, along(-2, inner))

    first, sums = cross_part(near_rows, far_rows, sums, x1, z1, single)
    sums, swapped = lax.optimization_barrier((sums[:, 0], swapped))
    steps = [1 << n for n in range(lax.axis_size(AXES).bit_length() - 1)]
    sums = sum_over(sums, steps[:1] + steps[4:] + steps[1:3])
    partial = mid_part(own, near_rows, far_rows, first, swapped)
    partial, sums = lax.optimization_barrier((partial, sums))
    away, *pairs = away_part(near_rows, partial, x1, x2, z1, z2, g, h, single)
    came = to_partner(away)
    out = near_part(mask, near_rows, partial, inside, *pairs)
    traces = sum_over(sums, steps[3:4])
    square = join(mask, came, out)
    return square, traces


def solution(mesh):
    return jax.shard_map(
        body,
        mesh=mesh,
        in_specs=(P(AXES, None, None, None), P(AXES, None), P(AXES)),
        out_specs=(P(AXES, None, None, None), P()),
        check_vma=False,
    )
```

```python
import jax
import jax.numpy as jnp
from jax import lax
from jax.experimental import pallas as pl
from jax.experimental.pallas import tpu as pltpu
from jax.sharding import PartitionSpec as P

AXES = ("row", "col")
HALF = 13
BAND = 2 * HALF + 1
BS = 128
NEAR = HALF
FAR = 12
NCOL = NEAR + 1
NEAR_W, OWN_W, FAR_W = NCOL * BS, 4 * BS, FAR * BS
OWN_AT, FAR_AT = NEAR_W, NEAR_W + OWN_W
VMEM_LIMIT = 20 * 1024 * 1024

VM = pl.BlockSpec(memory_space=pltpu.VMEM)
SM = pl.BlockSpec(memory_space=pltpu.SMEM)
HB = pl.BlockSpec(memory_space=pl.ANY)


def params():
    return pltpu.CompilerParams(vmem_limit_bytes=VMEM_LIMIT)


def permute(value, target):
    devices = lax.axis_size(AXES)
    pairs = [(i, target(i)) for i in range(devices)]
    return lax.ppermute(value, AXES, [(i, j) for i, j in pairs if 0 <= j < devices])


def to_partner(value):
    return permute(value, lambda i: i ^ 1)


def to_side(value, distance, senders=lambda i: True):
    def target(i):
        chip, core = divmod(i, 2)
        if not senders(i):
            return -1
        return 2 * (chip + distance) if core else 2 * (chip - distance) + 1

    return permute(value, target)


def inner(i):
    return (i // 2 + i % 2) % 2 == 1


def sum_over(value, steps):
    for step in steps:
        value = value + permute(value, lambda i: i ^ step)
    return value


def nn(a, b):
    return lax.dot_general(a, b, (((1,), (0,)), ((), ())), preferred_element_type=jnp.float32)


def nt(a, b):
    return lax.dot_general(a, b, (((1,), (1,)), ((), ())), preferred_element_type=jnp.float32)


def cut(i, n=1):
    return slice(i * BS, (i + n) * BS)


def my_core():
    return lax.rem(lax.axis_index("col"), 2)


def faces_pair():
    index = lax.axis_index("row") * lax.axis_size("col") + lax.axis_index("col")
    return lax.rem(lax.div(index, 2) + lax.rem(index, 2), 2) > 0


def own_kernel(table, blocks, mine, soon, later, mask, flags):
    core = my_core()
    first_row = 2 * (lax.axis_index("row") * lax.axis_size("col") + lax.axis_index("col"))
    for r in range(2):
        for w in range(BAND):
            flags[r, w] = 0
    for r in range(2):

        @pl.loop(0, table[2, r])
        def _(n):
            flags[r, table[r, n] - first_row - r + HALF] = 1

    def block(e, w):
        r = jnp.where(core > 0, 1 - e, e)
        a = jnp.where(core > 0, BAND - 1 - w, w)
        return jnp.where(flags[r, a] > 0, blocks[r, a], jnp.zeros((BS, BS), blocks.dtype))

    for r in range(2):
        for a in range(BAND):
            mask[r, a] = jnp.full((1, BS), flags[r, a], jnp.int32)
    for p in range(2):
        for w in range(BAND):
            mine[p, w] = block(p, w)
    for out, first in ((soon, True), (later, False)):
        for n, (p, w) in enumerate(part_slots(first)):
            out[n] = block(1 - p, BAND - 1 - w)


def part_slots(first):
    soon = [set(range(9 - e)) | set(range(HALF, BAND - 1 - e)) | {HALF - 1 - e} for e in (2, 3)]
    return [(p, w) for p in range(2) for w in range(BAND) if (w in soon[p]) == first]


def own_rows(table, blocks):
    shape = jax.ShapeDtypeStruct(blocks.shape, blocks.dtype)
    parts = [
        jax.ShapeDtypeStruct((len(part_slots(first)), BS, BS), blocks.dtype)
        for first in (True, False)
    ]
    return pl.pallas_call(
        own_kernel,
        out_shape=(shape, *parts, jax.ShapeDtypeStruct((2, BAND, 1, BS), jnp.int32)),
        in_specs=[SM, VM],
        out_specs=(VM,) * 4,
        scratch_shapes=[pltpu.SMEM((2, BAND), jnp.int32)],
        compiler_params=params(),
        name="own_rows",
    )(table, blocks)


def low_slots(e):
    return [w for w in range(HALF, BAND - 1 - e) if e < 3 or not 5 <= w - HALF + 1 + e <= 8]


def first_kernel(mine, soon, x1, z1, z2, single):
    at = {}

    def put(out, e, slots):
        for w in slots:
            n = at.get(id(out), 0)
            out[n] = mine[e, w] if e < 2 else soon[part_slots(True).index((e - 2, w))]
            at[id(out)] = n + 1

    for e in range(4):
        put(x1, e, range(9 - e))
    for e in range(4):
        put(z1, e, range(5 - e))
    for e in range(4):
        put(z2, e, range(HALF, BAND - 5 - e))
    for e in range(4):
        put(x1, e, low_slots(e))
    for e in range(4):
        put(z1, e, range(HALF, BAND - 1 - e))
    for e in range(4):
        put(z1, e, range(HALF - 1 - e, HALF - e))
        put(z2, e, range(HALF - 1 - e, HALF - e))
    single[0] = jnp.where(faces_pair(), mine[0, 0], soon[part_slots(True).index((1, HALF))])


def first_packs(mine, soon):
    return pl.pallas_call(
        first_kernel,
        out_shape=[jax.ShapeDtypeStruct((n, BS, BS), mine.dtype) for n in (72, 64, 34, 1)],
        in_specs=[VM] * 2,
        out_specs=[VM] * 4,
        compiler_params=params(),
        name="first_packs",
    )(mine, soon)


def second_kernel(x1, z1, _, x2, g, h):
    at1 = at2 = 0
    start_x, start_z = 30, 14
    for e in range(4):
        for w in low_slots(e):
            x2[at1] = z1[start_z + w - HALF]
            at1 += 1
        for n in range(5 - e):
            g[at2] = z1[start_z + n]
            h[at2] = x1[start_x + n] if n < 4 - e or e < 3 else turned(z1[60])
            at2 += 1
        start_x += len(low_slots(e))
        start_z += 13 - e
    h[at2] = z1[14]


def second_packs(x1, z1, sums):
    return pl.pallas_call(
        second_kernel,
        out_shape=[jax.ShapeDtypeStruct((n, BS, BS), x1.dtype) for n in (42, 14, 15)],
        in_specs=[VM] * 3,
        out_specs=[VM] * 3,
        compiler_params=params(),
        name="second_packs",
    )(x1, z1, sums)


def join_cross_kernel(x1, z1, single, _, cross):
    for n in range(30):
        cross[n] = x1[n]
    for n in range(14):
        cross[30 + n] = z1[n]
    cross[44] = single[0]


def join_cross(x1, z1, single, sums):
    return pl.pallas_call(
        join_cross_kernel,
        out_shape=jax.ShapeDtypeStruct((45, BS, BS), x1.dtype),
        in_specs=[VM] * 4,
        out_specs=VM,
        compiler_params=params(),
        name="join_cross",
    )(x1, z1, single, sums)


def turned(x):
    return jnp.transpose(x.astype(jnp.float32)).astype(x.dtype)


def fill_rows(mine, soon, later, rows):
    zero = jnp.zeros((BS, BS), rows.dtype)

    def block(e, k):
        w = k - e + HALF
        if not 0 <= w < BAND:
            return zero
        if e < 2:
            return mine[e, w]
        for part, first in ((soon, True), (later, False)):
            if (e - 2, w) in part_slots(first):
                return part[part_slots(first).index((e - 2, w))]

    for e in range(4):
        for t in range(1, NCOL + 1):
            rows[cut(e), cut(t - 1)] = block(e, -t)
        for k in range(4):
            rows[cut(e), OWN_AT + k * BS : OWN_AT + (k + 1) * BS] = block(e, k)
        for u in range(1, FAR + 1):
            rows[cut(e), FAR_AT + (u - 1) * BS : FAR_AT + u * BS] = block(e, 3 + u)


def fill_pairs(block, near, low, pairs):
    for t in near:
        for s in range(low, NCOL + 1):
            if s > NEAR:
                x = jnp.zeros((BS, BS), pairs.dtype)
            else:
                x = turned(block(s, t)) if s < t else block(t, s)
            pairs[cut(t - low), cut(s - low)] = x


def near_start(t):
    first = 4 * ((t - 1) // 4) + 1
    return sum(14 - s for s in range(first, t))


def cross_start(t):
    return sum(10 - s for s in range(1, t))


def own_kernel_products(mine, soon, later, own_rows, inner, near_rows, far_rows, sums, rows):
    fill_rows(mine, soon, later, rows)
    own_rows[...] = rows[:, OWN_AT:FAR_AT]
    near_rows[...] = rows[:, :NEAR_W]
    far_rows[...] = rows[:, FAR_AT : FAR_AT + 10 * BS]
    own = rows[:, OWN_AT:FAR_AT]
    third = jnp.zeros((1, 1), jnp.float32)
    for c in range(NCOL // 2):
        near = rows[:, cut(2 * c, 2)]
        value = nn(own, near)
        third += jnp.sum(near.astype(jnp.float32) * value, keepdims=True)
    third = 3.0 * third
    top = rows[: 2 * BS, OWN_AT:FAR_AT]
    third += jnp.sum(top.astype(jnp.float32) * nn(top, own), keepdims=True)
    inner[...] = nt(rows[: 2 * BS, :], rows[...])
    second = jnp.zeros((1, 1), jnp.float32)
    for e in range(2):
        for w in range(BAND):
            x = mine[e, w].astype(jnp.float32)
            second += jnp.sum(x * x, keepdims=True)
    sums[0:1, :] = jnp.broadcast_to(second, (1, BS))
    sums[1:2, :] = jnp.broadcast_to(third, (1, BS))


def own_part(mine, soon, later):
    return pl.pallas_call(
        own_kernel_products,
        out_shape=(
            jax.ShapeDtypeStruct((4 * BS, OWN_W), mine.dtype),
            jax.ShapeDtypeStruct((2 * BS, OWN_W), jnp.float32),
            jax.ShapeDtypeStruct((4 * BS, NEAR_W), mine.dtype),
            jax.ShapeDtypeStruct((4 * BS, 10 * BS), mine.dtype),
            jax.ShapeDtypeStruct((2, BS), jnp.float32),
        ),
        in_specs=[VM] * 3,
        out_specs=(VM,) * 5,
        scratch_shapes=[pltpu.VMEM((4 * BS, FAR_AT + FAR_W), mine.dtype)],
        compiler_params=params(),
        cost_estimate=pl.CostEstimate(flops=2 * 10**9, bytes_accessed=10**6, transcendentals=0),
        name="own_part",
    )(mine, soon, later)


def fill_cross(block, pairs):
    for c in range(5):
        for g in range(5 - c):
            for n in (2 * c + 1, 2 * c + 2):
                for m in (2 * g + 1, 2 * g + 2):
                    x = block(n, m) if n + m <= 10 else jnp.zeros((BS, BS), pairs.dtype)
                    pairs[cut(n - 1), cut(m - 1)] = x


def cross_kernel(near_rows, far_rows, before, x1, z1, single, first, sums, pairs):
    def block(t, u):
        at = cross_start(t) + 10 - t - u
        if t == 9:
            return jnp.where(faces_pair(), single[0], jnp.zeros((BS, BS), pairs.dtype))
        return x1[at] if t < 5 else z1[at - 30]

    fill_cross(block, pairs)
    third = jnp.zeros((1, 1), jnp.float32)
    for c in range(5):
        at = cut(2 * c, 2)
        width = (10 - 2 * c) * BS
        value = nt(far_rows[:, :width], pairs[at, :width])
        first[:, at] = value
        third += jnp.sum(near_rows[:, at].astype(jnp.float32) * value, keepdims=True)
    scale = 1.0 / (2 * BS * lax.axis_size(AXES))
    sums[0:1, :] = before[0:1, :] * scale
    sums[1:2, :] = (before[1:2, :] + 6.0 * third) * scale


def cross_part(near_rows, far_rows, before, x1, z1, single):
    return pl.pallas_call(
        cross_kernel,
        out_shape=(
            jax.ShapeDtypeStruct((4 * BS, 10 * BS), jnp.float32),
            jax.ShapeDtypeStruct(before.shape, jnp.float32),
        ),
        in_specs=[VM] * 6,
        out_specs=(VM,) * 2,
        scratch_shapes=[pltpu.VMEM((10 * BS, 10 * BS), x1.dtype)],
        compiler_params=params(),
        cost_estimate=pl.CostEstimate(flops=10**9, bytes_accessed=10**6, transcendentals=0),
        name="cross_part",
    )(near_rows, far_rows, before, x1, z1, single)


def mid_kernel(own, near_rows, far_rows, first, swapped, partial, cross):
    fill_cross(lambda u, t: swapped[cross_start(u) + 10 - t - u], cross)
    for c in range(NCOL // 2):
        at = cut(2 * c, 2)
        value = nn(own[...], near_rows[:, at])
        if c < 5:
            width = (10 - 2 * c) * BS
            value += first[:, at]
            value += nn(far_rows[:, :width], cross[:width, at])
        partial[:, at] = value


def mid_part(own, near_rows, far_rows, first, swapped):
    return pl.pallas_call(
        mid_kernel,
        out_shape=jax.ShapeDtypeStruct(near_rows.shape, jnp.float32),
        in_specs=[VM] * 5,
        out_specs=VM,
        scratch_shapes=[pltpu.VMEM((10 * BS, 10 * BS), near_rows.dtype)],
        compiler_params=params(),
        cost_estimate=pl.CostEstimate(flops=2 * 10**9, bytes_accessed=10**6, transcendentals=0),
        name="mid_part",
    )(own, near_rows, far_rows, first, swapped)


LOW, LAST = 5, 9


def fill_near(facing, x1, x2, z1, z2, g, h, single, pairs1, pairs2, pairs3):
    def block(t, s):
        if t == NEAR:
            return jnp.where(facing, h[14], single[0])
        if t >= LAST:
            at = near_start(t) + s - t
            return jnp.where(facing, h[at], g[at])
        if t >= LOW:
            start = 14 + sum(13 - n for n in range(t - LOW))
            return jnp.where(facing, z1[start + s - t], z2[near_start(t) + s - t])
        if t == 4 and LOW <= s < LAST:
            at = s - LOW
            return turned(jnp.where(facing, z1[60 + at], z2[30 + at]))
        slots = low_slots(t - 1)
        at = sum(len(low_slots(n)) for n in range(t - 1)) + slots.index(HALF + s - t)
        return jnp.where(facing, x1[30 + at], x2[at])

    fill_pairs(block, range(1, LOW), 1, pairs1)
    fill_pairs(block, range(LOW, LAST), LOW, pairs2)
    fill_pairs(block, range(LAST, NEAR + 1), LAST, pairs3)
    pairs3[cut(NCOL - LAST), :] = jnp.zeros((BS, (NCOL + 1 - LAST) * BS), pairs3.dtype)


def near_products(half, near_rows, partial, pairs1, pairs2, pairs3):
    rows = slice(2 * half * BS, (2 * half + 2) * BS)
    two, three = (LOW - 1) * BS, (LAST - 1) * BS
    for c in range(NCOL // 2):
        at = 2 * c * BS
        to = at + 2 * BS
        value = partial[rows, at:to]
        if at < two:
            value += nt(near_rows[rows, :], pairs1[at:to, :])
        else:
            value += nn(near_rows[rows, :two], pairs1[:, at:to])
        if two <= at < three:
            value += nt(near_rows[rows, two:], pairs2[at - two : to - two, :])
        elif at >= three:
            value += nn(near_rows[rows, two:three], pairs2[:, at - two : to - two])
            value += nt(near_rows[rows, three:], pairs3[at - three : to - three, :])
        for n in range(2):
            t = 2 * c + 1 + n
            for e in range(2):
                if 2 * half + e + t <= HALF:
                    yield e, t, value[cut(e), cut(n)]


def away_kernel(near_rows, partial, x1, x2, z1, z2, g, h, single, away, pairs1, pairs2, pairs3):
    fill_near(faces_pair(), x1, x2, z1, z2, g, h, single, pairs1, pairs2, pairs3)
    for e, t, value in near_products(1, near_rows, partial, pairs1, pairs2, pairs3):
        away[e * 11 + t - 1] = value.astype(away.dtype)


def away_part(near_rows, partial, x1, x2, z1, z2, g, h, single):
    shapes = (21, BS, BS), (4 * BS, NEAR_W), (4 * BS, 10 * BS), (6 * BS, 6 * BS)
    return pl.pallas_call(
        away_kernel,
        out_shape=[jax.ShapeDtypeStruct(shape, x1.dtype) for shape in shapes],
        in_specs=[VM] * 9,
        out_specs=[VM] * 4,
        compiler_params=params(),
        cost_estimate=pl.CostEstimate(flops=2 * 10**9, bytes_accessed=10**6, transcendentals=0),
        name="away_part",
    )(near_rows, partial, x1, x2, z1, z2, g, h, single)


def near_kernel(mask, near_rows, partial, inner, pairs1, pairs2, pairs3, out, held, sems):
    core = my_core()
    copies = []

    def put(e, w, value):
        r = jnp.where(core > 0, 1 - e, e)
        a = jnp.where(core > 0, BAND - 1 - w, w)
        held[r, a] = jnp.where(mask[r, a] > 0, value, 0.0).astype(held.dtype)

    def send(e, lo, n):
        r = jnp.where(core > 0, 1 - e, e)
        part = pl.ds(jnp.where(core > 0, BAND - lo - n, lo), n)
        copy = pltpu.make_async_copy(held.at[r, part], out.at[r, part], sems.at[len(copies)])
        copy.start()
        copies.append(copy)

    for e in range(2):
        for k in range(4):
            put(e, k - e + HALF, inner[cut(e), cut(k)])
        send(e, HALF - e, 4)
    for e, t, value in near_products(0, near_rows, partial, pairs1, pairs2, pairs3):
        put(e, HALF - e - t, value)
        if t % 2 == 0:
            send(e, HALF - e - t, 2)
        elif e + t == HALF:
            send(e, 0, 1)
    for copy in copies:
        copy.wait()


def near_part(mask, near_rows, partial, inner, *pairs):
    return pl.pallas_call(
        near_kernel,
        out_shape=jax.ShapeDtypeStruct((2, BAND, BS, BS), near_rows.dtype),
        in_specs=[VM] * 7,
        out_specs=HB,
        scratch_shapes=[
            pltpu.VMEM((2, BAND, BS, BS), near_rows.dtype),
            pltpu.SemaphoreType.DMA((16,)),
        ],
        compiler_params=params(),
        cost_estimate=pl.CostEstimate(flops=10**9, bytes_accessed=10**6, transcendentals=0),
        name="near_part",
    )(mask, near_rows, partial, inner, *pairs)


def join_kernel(mask, came, _, out, held, sems):
    core = my_core()
    copies = []
    for e, count, base in ((0, 10, 11), (1, 11, 0)):
        r = jnp.where(core > 0, 1 - e, e)

        @pl.loop(0, count)
        def _(n):
            w = BAND - count + n
            a = jnp.where(core > 0, BAND - 1 - w, w)
            spot = jnp.where(core > 0, count - 1 - n, n)
            x = came[base + n]
            held[base + spot] = jnp.where(mask[r, a] > 0, x, jnp.zeros_like(x))

        start = jnp.where(core > 0, 0, BAND - count)
        copy = pltpu.make_async_copy(
            held.at[pl.ds(base, count)], out.at[r, pl.ds(start, count)], sems.at[e]
        )
        copy.start()
        copies.append(copy)
    for copy in copies:
        copy.wait()


def join(mask, came, out):
    anywhere = pl.BlockSpec(memory_space=pl.ANY)
    return pl.pallas_call(
        join_kernel,
        out_shape=jax.ShapeDtypeStruct(out.shape, out.dtype),
        in_specs=[VM, VM, anywhere],
        out_specs=anywhere,
        scratch_shapes=[
            pltpu.VMEM(came.shape, came.dtype),
            pltpu.SemaphoreType.DMA((2,)),
        ],
        input_output_aliases={2: 0},
        compiler_params=params(),
        name="join",
    )(mask, came, out)


def body(blocks, columns, counts):
    table = jnp.pad(columns, ((0, 1), (0, 0))) + jnp.pad(counts[None], ((2, 0), (0, BAND - 2)))
    mine, soon, later, mask = own_rows(table, blocks)
    soon, later = to_partner(soon), to_partner(later)

    def outer(i):
        return not inner(i)

    x1, z1, z2, single = first_packs(mine, soon)
    x1 = to_side(x1, 1, inner)
    z1 = to_side(z1, 2, outer)

    def singles(i):
        chip, core = divmod(i, 2)
        if inner(i):
            return 2 * (chip + 3) if core else 2 * (chip - 3) + 1
        return 2 * (chip - 4) + 1 if core else 2 * (chip + 4)

    single = permute(single, singles)
    own, inside, near_rows, far_rows, sums = own_part(mine, soon, later)

    x2, g, h = second_packs(x1, z1, sums)
    swapped = permute(join_cross(x1, z1, single, g), lambda i: i ^ 1 if inner(i) else -1)

    def along(pair, senders):
        def target(i):
            chip, core = divmod(i, 2)
            return 2 * (chip + (pair if core else -pair)) + core if senders(i) else -1

        return target

    z2 = to_side(z2, 2, inner)
    x2 = permute(x2, along(1, inner))
    g = permute(g, along(-1, inner))
    h = permute(h, along(-2, inner))

    first, sums = cross_part(near_rows, far_rows, sums, x1, z1, single)
    sums, swapped = lax.optimization_barrier((sums[:, 0], swapped))
    steps = [1 << n for n in range(lax.axis_size(AXES).bit_length() - 1)]
    sums = sum_over(sums, steps[:1] + steps[4:] + steps[1:2] + steps[3:4])
    partial = mid_part(own, near_rows, far_rows, first, swapped)
    partial, sums = lax.optimization_barrier((partial, sums))
    away, *pairs = away_part(near_rows, partial, x1, x2, z1, z2, g, h, single)
    came = to_partner(away)
    out = near_part(mask, near_rows, partial, inside, *pairs)
    traces = sum_over(sums, steps[2:3])
    square = join(mask, came, out)
    return square, traces


def solution(mesh):
    return jax.shard_map(
        body,
        mesh=mesh,
        in_specs=(P(AXES, None, None, None), P(AXES, None), P(AXES)),
        out_specs=(P(AXES, None, None, None), P()),
        check_vma=False,
    )
```

```python
import jax
import jax.numpy as jnp
from jax import lax
from jax.experimental import pallas as pl
from jax.experimental.pallas import tpu as pltpu
from jax.sharding import PartitionSpec as P

AXES = ("row", "col")
HALF = 13
BAND = 2 * HALF + 1
BS = 128
NEAR = HALF
FAR = 12
NCOL = NEAR + 1
NEAR_W, OWN_W, FAR_W = NCOL * BS, 4 * BS, FAR * BS
OWN_AT, FAR_AT = NEAR_W, NEAR_W + OWN_W
VMEM_LIMIT = 20 * 1024 * 1024

VM = pl.BlockSpec(memory_space=pltpu.VMEM)
SM = pl.BlockSpec(memory_space=pltpu.SMEM)
HB = pl.BlockSpec(memory_space=pl.ANY)


def params():
    return pltpu.CompilerParams(vmem_limit_bytes=VMEM_LIMIT)


def permute(value, target):
    devices = lax.axis_size(AXES)
    pairs = [(i, target(i)) for i in range(devices)]
    return lax.ppermute(value, AXES, [(i, j) for i, j in pairs if 0 <= j < devices])


def to_partner(value):
    return permute(value, lambda i: i ^ 1)


def to_side(value, distance, senders=lambda i: True):
    def target(i):
        chip, core = divmod(i, 2)
        if not senders(i):
            return -1
        return 2 * (chip + distance) if core else 2 * (chip - distance) + 1

    return permute(value, target)


def inner(i):
    return (i // 2 + i % 2) % 2 == 1


def sum_over(value, steps):
    for step in steps:
        value = value + permute(value, lambda i: i ^ step)
    return value


def nn(a, b):
    return lax.dot_general(a, b, (((1,), (0,)), ((), ())), preferred_element_type=jnp.float32)


def nt(a, b):
    return lax.dot_general(a, b, (((1,), (1,)), ((), ())), preferred_element_type=jnp.float32)


def cut(i, n=1):
    return slice(i * BS, (i + n) * BS)


def my_core():
    return lax.rem(lax.axis_index("col"), 2)


def faces_pair():
    index = lax.axis_index("row") * lax.axis_size("col") + lax.axis_index("col")
    return lax.rem(lax.div(index, 2) + lax.rem(index, 2), 2) > 0


def own_kernel(table, blocks, mine, other, mask, flags):
    core = my_core()
    first_row = 2 * (lax.axis_index("row") * lax.axis_size("col") + lax.axis_index("col"))
    for r in range(2):
        for w in range(BAND):
            flags[r, w] = 0
    for r in range(2):

        @pl.loop(0, table[2, r])
        def _(n):
            flags[r, table[r, n] - first_row - r + HALF] = 1

    for r in range(2):
        e = jnp.where(core > 0, 1 - r, r)
        for a in range(BAND):
            keep = flags[r, a]
            mask[r, a] = jnp.full((1, BS), keep, jnp.int32)
            x = jnp.where(keep > 0, blocks[r, a], jnp.zeros((BS, BS), blocks.dtype))
            w = jnp.where(core > 0, BAND - 1 - a, a)
            mine[e, w] = x
            other[1 - e, BAND - 1 - w] = x


def own_rows(table, blocks):
    shape = jax.ShapeDtypeStruct(blocks.shape, blocks.dtype)
    return pl.pallas_call(
        own_kernel,
        out_shape=(shape, shape, jax.ShapeDtypeStruct((2, BAND, 1, BS), jnp.int32)),
        in_specs=[SM, VM],
        out_specs=(VM, VM, VM),
        scratch_shapes=[pltpu.SMEM((2, BAND), jnp.int32)],
        compiler_params=params(),
        name="own_rows",
    )(table, blocks)


def low_slots(e):
    return [w for w in range(HALF, BAND - 1 - e) if e < 3 or not 5 <= w - HALF + 1 + e <= 8]


def first_kernel(mine, part, x1, z1, z2, corner, diagonal):
    at = {}

    def put(out, e, slots):
        for w in slots:
            n = at.get(id(out), 0)
            out[n] = mine[e, w] if e < 2 else part[e - 2, w]
            at[id(out)] = n + 1

    for e in range(4):
        put(x1, e, range(9 - e))
    for e in range(4):
        put(z1, 3 - e, range(BAND - 1, BAND - 6 + e, -1))
    for e in range(4):
        put(z2, e, range(HALF, BAND - 5 - e))
    for e in range(4):
        put(x1, e, low_slots(e))
    for e in range(4):
        put(z1, 3 - e, range(HALF, e, -1))
    for e in range(4):
        put(z1, 3 - e, [HALF + 1 + e])
        put(z2, e, [HALF - 1 - e])
    corner[0] = part[1, BAND - 1]
    diagonal[0] = part[1, HALF]


def first_packs(mine, part):
    return pl.pallas_call(
        first_kernel,
        out_shape=[jax.ShapeDtypeStruct((n, BS, BS), mine.dtype) for n in (72, 64, 34, 1, 1)],
        in_specs=[VM] * 2,
        out_specs=[VM] * 5,
        compiler_params=params(),
        name="first_packs",
    )(mine, part)


def second_kernel(x1, z1, _sums, _diagonal, x2, g, h):
    at1 = at2 = 0
    start_x, start_z = 30, 14
    for e in range(4):
        for w in low_slots(e):
            x2[at1] = z1[start_z + w - HALF]
            at1 += 1
        for n in range(5 - e):
            g[at2] = z1[start_z + n]
            h[at2] = x1[start_x + n] if n < 4 - e or e < 3 else turned(z1[60])
            at2 += 1
        start_x += len(low_slots(e))
        start_z += 13 - e
    h[at2] = z1[14]


def second_packs(x1, z1, sums, diagonal):
    return pl.pallas_call(
        second_kernel,
        out_shape=[jax.ShapeDtypeStruct((n, BS, BS), x1.dtype) for n in (42, 14, 15)],
        in_specs=[VM] * 4,
        out_specs=[VM] * 3,
        compiler_params=params(),
        name="second_packs",
    )(x1, z1, sums, diagonal)


def join_cross_kernel(x1, z1, single, _, cross):
    for n in range(30):
        cross[n] = x1[n]
    for n in range(14):
        cross[30 + n] = z1[n]
    cross[44] = single[0]


def join_cross(x1, z1, single, sums):
    return pl.pallas_call(
        join_cross_kernel,
        out_shape=jax.ShapeDtypeStruct((45, BS, BS), x1.dtype),
        in_specs=[VM] * 4,
        out_specs=VM,
        compiler_params=params(),
        name="join_cross",
    )(x1, z1, single, sums)


def turned(x):
    return jnp.transpose(x.astype(jnp.float32)).astype(x.dtype)


def fill_rows(mine, part, rows):
    zero = jnp.zeros((BS, BS), rows.dtype)

    def block(e, k):
        w = k - e + HALF
        if not 0 <= w < BAND:
            return zero
        return mine[e, w] if e < 2 else part[e - 2, w]

    for e in range(4):
        for t in range(1, NCOL + 1):
            rows[cut(e), cut(t - 1)] = block(e, -t)
        for k in range(4):
            rows[cut(e), OWN_AT + k * BS : OWN_AT + (k + 1) * BS] = block(e, k)
        for u in range(1, FAR + 1):
            rows[cut(e), FAR_AT + (u - 1) * BS : FAR_AT + u * BS] = block(e, 3 + u)


def fill_pairs(block, near, low, pairs):
    for t in near:
        for s in range(low, NCOL + 1):
            if s > NEAR:
                x = jnp.zeros((BS, BS), pairs.dtype)
            else:
                x = turned(block(s, t)) if s < t else block(t, s)
            pairs[cut(t - low), cut(s - low)] = x


def near_start(t):
    first = 4 * ((t - 1) // 4) + 1
    return sum(14 - s for s in range(first, t))


def cross_start(t):
    return sum(10 - s for s in range(1, t))


def own_kernel_products(mine, part, own_rows, inner, near_rows, far_rows, sums, rows):
    fill_rows(mine, part, rows)
    own_rows[...] = rows[:, OWN_AT:FAR_AT]
    near_rows[...] = rows[:, :NEAR_W]
    far_rows[...] = rows[:, FAR_AT : FAR_AT + 10 * BS]
    own = rows[:, OWN_AT:FAR_AT]
    third = jnp.zeros((1, 1), jnp.float32)
    for c in range(NCOL // 2):
        near = rows[:, cut(2 * c, 2)]
        value = nn(own, near)
        third += jnp.sum(near.astype(jnp.float32) * value, keepdims=True)
    third = 3.0 * third
    top = rows[: 2 * BS, OWN_AT:FAR_AT]
    third += jnp.sum(top.astype(jnp.float32) * nn(top, own), keepdims=True)
    inner[...] = nt(rows[: 2 * BS, :], rows[...])
    second = jnp.zeros((1, 1), jnp.float32)
    for e in range(2):
        for w in range(BAND):
            x = mine[e, w].astype(jnp.float32)
            second += jnp.sum(x * x, keepdims=True)
    sums[0:1, :] = jnp.broadcast_to(second, (1, BS))
    sums[1:2, :] = jnp.broadcast_to(third, (1, BS))


def own_part(mine, part):
    return pl.pallas_call(
        own_kernel_products,
        out_shape=(
            jax.ShapeDtypeStruct((4 * BS, OWN_W), mine.dtype),
            jax.ShapeDtypeStruct((2 * BS, OWN_W), jnp.float32),
            jax.ShapeDtypeStruct((4 * BS, NEAR_W), mine.dtype),
            jax.ShapeDtypeStruct((4 * BS, 10 * BS), mine.dtype),
            jax.ShapeDtypeStruct((2, BS), jnp.float32),
        ),
        in_specs=[VM] * 2,
        out_specs=(VM,) * 5,
        scratch_shapes=[pltpu.VMEM((4 * BS, FAR_AT + FAR_W), mine.dtype)],
        compiler_params=params(),
        cost_estimate=pl.CostEstimate(flops=2 * 10**9, bytes_accessed=10**6, transcendentals=0),
        name="own_part",
    )(mine, part)


def fill_cross(block, pairs):
    for c in range(5):
        for g in range(5 - c):
            for n in (2 * c + 1, 2 * c + 2):
                for m in (2 * g + 1, 2 * g + 2):
                    x = block(n, m) if n + m <= 10 else jnp.zeros((BS, BS), pairs.dtype)
                    pairs[cut(n - 1), cut(m - 1)] = x


def cross_kernel(near_rows, far_rows, before, x1, z1, single, _diagonal, first, sums, pairs):
    def block(t, u):
        at = cross_start(t) + 10 - t - u
        if t == 9:
            return jnp.where(faces_pair(), single[0], jnp.zeros((BS, BS), pairs.dtype))
        return x1[at] if t < 5 else z1[at - 30]

    fill_cross(block, pairs)
    third = jnp.zeros((1, 1), jnp.float32)
    for c in range(5):
        at = cut(2 * c, 2)
        width = (10 - 2 * c) * BS
        value = nt(far_rows[:, :width], pairs[at, :width])
        first[:, at] = value
        third += jnp.sum(near_rows[:, at].astype(jnp.float32) * value, keepdims=True)
    scale = 1.0 / (2 * BS * lax.axis_size(AXES))
    sums[0:1, :] = before[0:1, :] * scale
    sums[1:2, :] = (before[1:2, :] + 6.0 * third) * scale


def cross_part(near_rows, far_rows, before, x1, z1, single, diagonal):
    return pl.pallas_call(
        cross_kernel,
        out_shape=(
            jax.ShapeDtypeStruct((4 * BS, 10 * BS), jnp.float32),
            jax.ShapeDtypeStruct(before.shape, jnp.float32),
        ),
        in_specs=[VM] * 7,
        out_specs=(VM,) * 2,
        scratch_shapes=[pltpu.VMEM((10 * BS, 10 * BS), x1.dtype)],
        compiler_params=params(),
        cost_estimate=pl.CostEstimate(flops=10**9, bytes_accessed=10**6, transcendentals=0),
        name="cross_part",
    )(near_rows, far_rows, before, x1, z1, single, diagonal)


def mid_kernel(own, near_rows, far_rows, first, swapped, partial, cross):
    fill_cross(lambda u, t: swapped[cross_start(u) + 10 - t - u], cross)
    for c in range(NCOL // 2):
        at = cut(2 * c, 2)
        value = nn(own[...], near_rows[:, at])
        if c < 5:
            width = (10 - 2 * c) * BS
            value += first[:, at]
            value += nn(far_rows[:, :width], cross[:width, at])
        partial[:, at] = value


def mid_part(own, near_rows, far_rows, first, swapped):
    return pl.pallas_call(
        mid_kernel,
        out_shape=jax.ShapeDtypeStruct(near_rows.shape, jnp.float32),
        in_specs=[VM] * 5,
        out_specs=VM,
        scratch_shapes=[pltpu.VMEM((10 * BS, 10 * BS), near_rows.dtype)],
        compiler_params=params(),
        cost_estimate=pl.CostEstimate(flops=2 * 10**9, bytes_accessed=10**6, transcendentals=0),
        name="mid_part",
    )(own, near_rows, far_rows, first, swapped)


LOW, LAST = 5, 9


def fill_near(facing, x1, x2, z1, z2, g, h, single, pairs1, pairs2, pairs3):
    def block(t, s):
        if t == NEAR:
            return jnp.where(facing, h[14], single[0])
        if t >= LAST:
            at = near_start(t) + s - t
            return jnp.where(facing, h[at], g[at])
        if t >= LOW:
            start = 14 + sum(13 - n for n in range(t - LOW))
            return jnp.where(facing, z1[start + s - t], z2[near_start(t) + s - t])
        if t == 4 and LOW <= s < LAST:
            at = s - LOW
            return turned(jnp.where(facing, z1[60 + at], z2[30 + at]))
        slots = low_slots(t - 1)
        at = sum(len(low_slots(n)) for n in range(t - 1)) + slots.index(HALF + s - t)
        return jnp.where(facing, x1[30 + at], x2[at])

    fill_pairs(block, range(1, LOW), 1, pairs1)
    fill_pairs(block, range(LOW, LAST), LOW, pairs2)
    fill_pairs(block, range(LAST, NEAR + 1), LAST, pairs3)
    pairs3[cut(NCOL - LAST), :] = jnp.zeros((BS, (NCOL + 1 - LAST) * BS), pairs3.dtype)


def near_products(half, near_rows, partial, pairs1, pairs2, pairs3):
    rows = slice(2 * half * BS, (2 * half + 2) * BS)
    two, three = (LOW - 1) * BS, (LAST - 1) * BS
    for c in range(NCOL // 2):
        at = 2 * c * BS
        to = at + 2 * BS
        value = partial[rows, at:to]
        if at < two:
            value += nt(near_rows[rows, :], pairs1[at:to, :])
        else:
            value += nn(near_rows[rows, :two], pairs1[:, at:to])
        if two <= at < three:
            value += nt(near_rows[rows, two:], pairs2[at - two : to - two, :])
        elif at >= three:
            value += nn(near_rows[rows, two:three], pairs2[:, at - two : to - two])
            value += nt(near_rows[rows, three:], pairs3[at - three : to - three, :])
        for n in range(2):
            t = 2 * c + 1 + n
            for e in range(2):
                if 2 * half + e + t <= HALF:
                    yield e, t, value[cut(e), cut(n)]


def away_kernel(near_rows, partial, x1, x2, z1, z2, g, h, single, away, pairs1, pairs2, pairs3):
    fill_near(faces_pair(), x1, x2, z1, z2, g, h, single, pairs1, pairs2, pairs3)
    for e, t, value in near_products(1, near_rows, partial, pairs1, pairs2, pairs3):
        away[e * 11 + t - 1] = value.astype(away.dtype)


def away_part(near_rows, partial, x1, x2, z1, z2, g, h, single):
    shapes = (21, BS, BS), (4 * BS, NEAR_W), (4 * BS, 10 * BS), (6 * BS, 6 * BS)
    return pl.pallas_call(
        away_kernel,
        out_shape=[jax.ShapeDtypeStruct(shape, x1.dtype) for shape in shapes],
        in_specs=[VM] * 9,
        out_specs=[VM] * 4,
        compiler_params=params(),
        cost_estimate=pl.CostEstimate(flops=2 * 10**9, bytes_accessed=10**6, transcendentals=0),
        name="away_part",
    )(near_rows, partial, x1, x2, z1, z2, g, h, single)


def near_kernel(mask, near_rows, partial, inner, pairs1, pairs2, pairs3, out, held, sems):
    core = my_core()
    copies = []

    def put(e, w, value):
        r = jnp.where(core > 0, 1 - e, e)
        a = jnp.where(core > 0, BAND - 1 - w, w)
        held[r, a] = jnp.where(mask[r, a] > 0, value, 0.0).astype(held.dtype)

    def send(e, lo, n):
        r = jnp.where(core > 0, 1 - e, e)
        part = pl.ds(jnp.where(core > 0, BAND - lo - n, lo), n)
        copy = pltpu.make_async_copy(held.at[r, part], out.at[r, part], sems.at[len(copies)])
        copy.start()
        copies.append(copy)

    for e in range(2):
        for k in range(4):
            put(e, k - e + HALF, inner[cut(e), cut(k)])
        send(e, HALF - e, 4)
    for e, t, value in near_products(0, near_rows, partial, pairs1, pairs2, pairs3):
        put(e, HALF - e - t, value)
        if t % 2 == 0:
            send(e, HALF - e - t, 2)
        elif e + t == HALF:
            send(e, 0, 1)
    for copy in copies:
        copy.wait()


def near_part(mask, near_rows, partial, inner, *pairs):
    return pl.pallas_call(
        near_kernel,
        out_shape=jax.ShapeDtypeStruct((2, BAND, BS, BS), near_rows.dtype),
        in_specs=[VM] * 7,
        out_specs=HB,
        scratch_shapes=[
            pltpu.VMEM((2, BAND, BS, BS), near_rows.dtype),
            pltpu.SemaphoreType.DMA((16,)),
        ],
        compiler_params=params(),
        cost_estimate=pl.CostEstimate(flops=10**9, bytes_accessed=10**6, transcendentals=0),
        name="near_part",
    )(mask, near_rows, partial, inner, *pairs)


def join_kernel(mask, came, _, out, held, sems):
    core = my_core()
    copies = []
    for e, count, base in ((0, 10, 11), (1, 11, 0)):
        r = jnp.where(core > 0, 1 - e, e)

        @pl.loop(0, count)
        def _(n):
            w = BAND - count + n
            a = jnp.where(core > 0, BAND - 1 - w, w)
            spot = jnp.where(core > 0, count - 1 - n, n)
            x = came[base + n]
            held[base + spot] = jnp.where(mask[r, a] > 0, x, jnp.zeros_like(x))

        start = jnp.where(core > 0, 0, BAND - count)
        copy = pltpu.make_async_copy(
            held.at[pl.ds(base, count)], out.at[r, pl.ds(start, count)], sems.at[e]
        )
        copy.start()
        copies.append(copy)
    for copy in copies:
        copy.wait()


def join(mask, came, out):
    anywhere = pl.BlockSpec(memory_space=pl.ANY)
    return pl.pallas_call(
        join_kernel,
        out_shape=jax.ShapeDtypeStruct(out.shape, out.dtype),
        in_specs=[VM, VM, anywhere],
        out_specs=anywhere,
        scratch_shapes=[
            pltpu.VMEM(came.shape, came.dtype),
            pltpu.SemaphoreType.DMA((2,)),
        ],
        input_output_aliases={2: 0},
        compiler_params=params(),
        name="join",
    )(mask, came, out)


def body(blocks, columns, counts):
    table = jnp.pad(columns, ((0, 1), (0, 0))) + jnp.pad(counts[None], ((2, 0), (0, BAND - 2)))
    mine, other, mask = own_rows(table, blocks)
    part = to_partner(other)

    def outer(i):
        return not inner(i)

    x1, z1, z2, corner, diagonal = first_packs(mine, part)

    def along(pair, senders):
        def target(i):
            chip, core = divmod(i, 2)
            return 2 * (chip + (pair if core else -pair)) + core if senders(i) else -1

        return target

    x1 = to_side(x1, 1, inner)
    z1 = permute(z1, along(-2, inner))
    corner = permute(corner, along(-3, outer))
    diagonal = permute(diagonal, along(-4, outer))
    own, inside, near_rows, far_rows, sums = own_part(mine, part)

    x2, g, h = second_packs(x1, z1, sums, sums)
    swapped = permute(join_cross(x1, z1, corner, g), lambda i: i ^ 1 if inner(i) else -1)

    z2 = to_side(z2, 2, inner)
    x2 = permute(x2, along(1, inner))
    g = permute(g, along(-1, inner))
    h = permute(h, along(-2, inner))

    first, sums = cross_part(near_rows, far_rows, sums, x1, z1, corner, diagonal)
    sums, swapped = lax.optimization_barrier((sums[:, 0], swapped))
    steps = [1 << n for n in range(lax.axis_size(AXES).bit_length() - 1)]
    sums = sum_over(sums, steps[4:] + steps[:1] + steps[1:2] + steps[3:4])
    partial = mid_part(own, near_rows, far_rows, first, swapped)
    partial, sums = lax.optimization_barrier((partial, sums))
    away, *pairs = away_part(near_rows, partial, x1, x2, z1, z2, g, h, diagonal)
    came = to_partner(away)
    out = near_part(mask, near_rows, partial, inside, *pairs)
    traces = sum_over(sums, steps[2:3])
    square = join(mask, came, out)
    return square, traces


def solution(mesh):
    return jax.shard_map(
        body,
        mesh=mesh,
        in_specs=(P(AXES, None, None, None), P(AXES, None), P(AXES)),
        out_specs=(P(AXES, None, None, None), P()),
        check_vma=False,
    )
```

```python
import jax
import jax.numpy as jnp
from jax import lax
from jax.experimental import pallas as pl
from jax.experimental.pallas import tpu as pltpu
from jax.sharding import PartitionSpec as P

AXES = ("row", "col")
HALF = 13
BAND = 2 * HALF + 1
BS = 128
NEAR = HALF
MOVED = 2
FAR = 12
NCOL = NEAR + 1
NEAR_W, OWN_W, FAR_W = NCOL * BS, 4 * BS, FAR * BS
OWN_AT, FAR_AT = NEAR_W, NEAR_W + OWN_W
VMEM_LIMIT = 20 * 1024 * 1024

VM = pl.BlockSpec(memory_space=pltpu.VMEM)
SM = pl.BlockSpec(memory_space=pltpu.SMEM)
HB = pl.BlockSpec(memory_space=pl.ANY)


def params():
    return pltpu.CompilerParams(vmem_limit_bytes=VMEM_LIMIT)


def permute(value, target):
    devices = lax.axis_size(AXES)
    pairs = [(i, target(i)) for i in range(devices)]
    return lax.ppermute(value, AXES, [(i, j) for i, j in pairs if 0 <= j < devices])


def to_partner(value):
    return permute(value, lambda i: i ^ 1)


def to_side(value, distance, senders=lambda i: True):
    def target(i):
        chip, core = divmod(i, 2)
        if not senders(i):
            return -1
        return 2 * (chip + distance) if core else 2 * (chip - distance) + 1

    return permute(value, target)


def inner(i):
    return (i // 2 + i % 2) % 2 == 1


def sum_over(value, steps):
    for step in steps:
        value = value + permute(value, lambda i: i ^ step)
    return value


def nn(a, b):
    return lax.dot_general(a, b, (((1,), (0,)), ((), ())), preferred_element_type=jnp.float32)


def nt(a, b):
    return lax.dot_general(a, b, (((1,), (1,)), ((), ())), preferred_element_type=jnp.float32)


def cut(i, n=1):
    return slice(i * BS, (i + n) * BS)


def my_core():
    return lax.rem(lax.axis_index("col"), 2)


def faces_pair():
    index = lax.axis_index("row") * lax.axis_size("col") + lax.axis_index("col")
    return lax.rem(lax.div(index, 2) + lax.rem(index, 2), 2) > 0


def own_kernel(table, blocks, mine, other, mask, flags):
    core = my_core()
    first_row = 2 * (lax.axis_index("row") * lax.axis_size("col") + lax.axis_index("col"))
    for r in range(2):
        for w in range(BAND):
            flags[r, w] = 0
    for r in range(2):

        @pl.loop(0, table[2, r])
        def _(n):
            flags[r, table[r, n] - first_row - r + HALF] = 1

    for r in range(2):
        e = jnp.where(core > 0, 1 - r, r)
        for a in range(BAND):
            keep = flags[r, a]
            mask[r, a] = jnp.full((1, BS), keep, jnp.int32)
            x = jnp.where(keep > 0, blocks[r, a], jnp.zeros((BS, BS), blocks.dtype))
            w = jnp.where(core > 0, BAND - 1 - a, a)
            mine[e, w] = x
            other[1 - e, BAND - 1 - w] = x


def own_rows(table, blocks):
    shape = jax.ShapeDtypeStruct(blocks.shape, blocks.dtype)
    return pl.pallas_call(
        own_kernel,
        out_shape=(shape, shape, jax.ShapeDtypeStruct((2, BAND, 1, BS), jnp.int32)),
        in_specs=[SM, VM],
        out_specs=(VM, VM, VM),
        scratch_shapes=[pltpu.SMEM((2, BAND), jnp.int32)],
        compiler_params=params(),
        name="own_rows",
    )(table, blocks)


def low_slots(e):
    return [w for w in range(HALF, BAND - 1 - e) if e < 3 or not 5 <= w - HALF + 1 + e < 5 + MOVED]


def first_kernel(mine, part, x1, z1, z2, corner, diagonal):
    at = {}

    def put(out, e, slots):
        for w in slots:
            n = at.get(id(out), 0)
            out[n] = mine[e, w] if e < 2 else part[e - 2, w]
            at[id(out)] = n + 1

    for e in range(4):
        put(x1, e, range(9 - e))
    for e in range(4):
        put(z1, 3 - e, range(BAND - 1, BAND - 6 + e, -1))
    for e in range(4):
        put(z2, e, range(HALF, BAND - 5 - e))
    for e in range(4):
        put(x1, e, low_slots(e))
    for e in range(4):
        put(z1, 3 - e, range(HALF, e, -1))
    for e in range(MOVED):
        put(z1, 3 - e, [HALF + 1 + e])
        put(z2, e, [HALF - 1 - e])
    corner[0] = part[1, BAND - 1]
    diagonal[0] = part[1, HALF]


def first_packs(mine, part):
    return pl.pallas_call(
        first_kernel,
        out_shape=[jax.ShapeDtypeStruct((n, BS, BS), mine.dtype) for n in (76 - MOVED, 60 + MOVED, 30 + MOVED, 1, 1)],
        in_specs=[VM] * 2,
        out_specs=[VM] * 5,
        compiler_params=params(),
        name="first_packs",
    )(mine, part)


def second_kernel(x1, z1, _sums, _diagonal, x2, g, h):
    at1 = at2 = 0
    start_x, start_z = 30, 14
    for e in range(4):
        for w in low_slots(e):
            x2[at1] = z1[start_z + w - HALF]
            at1 += 1
        for n in range(5 - e):
            g[at2] = z1[start_z + n]
            h[at2] = x1[start_x + n] if n < 4 - e or e < 3 or not MOVED else turned(z1[60])
            at2 += 1
        start_x += len(low_slots(e))
        start_z += 13 - e
    h[at2] = z1[14]


def second_packs(x1, z1, sums, diagonal):
    return pl.pallas_call(
        second_kernel,
        out_shape=[jax.ShapeDtypeStruct((n, BS, BS), x1.dtype) for n in (46 - MOVED, 14, 15)],
        in_specs=[VM] * 4,
        out_specs=[VM] * 3,
        compiler_params=params(),
        name="second_packs",
    )(x1, z1, sums, diagonal)


def join_cross_kernel(x1, z1, single, _, cross):
    for n in range(30):
        cross[n] = x1[n]
    for n in range(14):
        cross[30 + n] = z1[n]
    cross[44] = single[0]


def join_cross(x1, z1, single, sums):
    return pl.pallas_call(
        join_cross_kernel,
        out_shape=jax.ShapeDtypeStruct((45, BS, BS), x1.dtype),
        in_specs=[VM] * 4,
        out_specs=VM,
        compiler_params=params(),
        name="join_cross",
    )(x1, z1, single, sums)


def turned(x):
    return jnp.transpose(x.astype(jnp.float32)).astype(x.dtype)


def fill_rows(mine, part, rows):
    zero = jnp.zeros((BS, BS), rows.dtype)

    def block(e, k):
        w = k - e + HALF
        if not 0 <= w < BAND:
            return zero
        return mine[e, w] if e < 2 else part[e - 2, w]

    for e in range(4):
        for t in range(1, NCOL + 1):
            rows[cut(e), cut(t - 1)] = block(e, -t)
        for k in range(4):
            rows[cut(e), OWN_AT + k * BS : OWN_AT + (k + 1) * BS] = block(e, k)
        for u in range(1, FAR + 1):
            rows[cut(e), FAR_AT + (u - 1) * BS : FAR_AT + u * BS] = block(e, 3 + u)


def fill_pairs(block, near, low, pairs):
    for t in near:
        for s in range(low, NCOL + 1):
            if s > NEAR:
                x = jnp.zeros((BS, BS), pairs.dtype)
            else:
                x = turned(block(s, t)) if s < t else block(t, s)
            pairs[cut(t - low), cut(s - low)] = x


def near_start(t):
    first = 4 * ((t - 1) // 4) + 1
    return sum(14 - s for s in range(first, t))


def cross_start(t):
    return sum(10 - s for s in range(1, t))


def own_kernel_products(mine, part, own_rows, inner, near_rows, far_rows, sums, rows):
    fill_rows(mine, part, rows)
    own_rows[...] = rows[:, OWN_AT:FAR_AT]
    near_rows[...] = rows[:, :NEAR_W]
    far_rows[...] = rows[:, FAR_AT : FAR_AT + 10 * BS]
    own = rows[:, OWN_AT:FAR_AT]
    third = jnp.zeros((1, 1), jnp.float32)
    for c in range(NCOL // 2):
        near = rows[:, cut(2 * c, 2)]
        value = nn(own, near)
        third += jnp.sum(near.astype(jnp.float32) * value, keepdims=True)
    third = 3.0 * third
    top = rows[: 2 * BS, OWN_AT:FAR_AT]
    third += jnp.sum(top.astype(jnp.float32) * nn(top, own), keepdims=True)
    inner[...] = nt(rows[: 2 * BS, :], rows[...])
    second = jnp.zeros((1, 1), jnp.float32)
    for e in range(2):
        for w in range(BAND):
            x = mine[e, w].astype(jnp.float32)
            second += jnp.sum(x * x, keepdims=True)
    sums[0:1, :] = jnp.broadcast_to(second, (1, BS))
    sums[1:2, :] = jnp.broadcast_to(third, (1, BS))


def own_part(mine, part):
    return pl.pallas_call(
        own_kernel_products,
        out_shape=(
            jax.ShapeDtypeStruct((4 * BS, OWN_W), mine.dtype),
            jax.ShapeDtypeStruct((2 * BS, OWN_W), jnp.float32),
            jax.ShapeDtypeStruct((4 * BS, NEAR_W), mine.dtype),
            jax.ShapeDtypeStruct((4 * BS, 10 * BS), mine.dtype),
            jax.ShapeDtypeStruct((2, BS), jnp.float32),
        ),
        in_specs=[VM] * 2,
        out_specs=(VM,) * 5,
        scratch_shapes=[pltpu.VMEM((4 * BS, FAR_AT + FAR_W), mine.dtype)],
        compiler_params=params(),
        cost_estimate=pl.CostEstimate(flops=2 * 10**9, bytes_accessed=10**6, transcendentals=0),
        name="own_part",
    )(mine, part)


def fill_cross(block, pairs):
    for c in range(5):
        for g in range(5 - c):
            for n in (2 * c + 1, 2 * c + 2):
                for m in (2 * g + 1, 2 * g + 2):
                    x = block(n, m) if n + m <= 10 else jnp.zeros((BS, BS), pairs.dtype)
                    pairs[cut(n - 1), cut(m - 1)] = x


def cross_kernel(near_rows, far_rows, before, x1, z1, single, _diagonal, first, sums, pairs):
    def block(t, u):
        at = cross_start(t) + 10 - t - u
        if t == 9:
            return jnp.where(faces_pair(), single[0], jnp.zeros((BS, BS), pairs.dtype))
        return x1[at] if t < 5 else z1[at - 30]

    fill_cross(block, pairs)
    third = jnp.zeros((1, 1), jnp.float32)
    for c in range(5):
        at = cut(2 * c, 2)
        width = (10 - 2 * c) * BS
        value = nt(far_rows[:, :width], pairs[at, :width])
        first[:, at] = value
        third += jnp.sum(near_rows[:, at].astype(jnp.float32) * value, keepdims=True)
    scale = 1.0 / (2 * BS * lax.axis_size(AXES))
    sums[0:1, :] = before[0:1, :] * scale
    sums[1:2, :] = (before[1:2, :] + 6.0 * third) * scale


def cross_part(near_rows, far_rows, before, x1, z1, single, diagonal):
    return pl.pallas_call(
        cross_kernel,
        out_shape=(
            jax.ShapeDtypeStruct((4 * BS, 10 * BS), jnp.float32),
            jax.ShapeDtypeStruct(before.shape, jnp.float32),
        ),
        in_specs=[VM] * 7,
        out_specs=(VM,) * 2,
        scratch_shapes=[pltpu.VMEM((10 * BS, 10 * BS), x1.dtype)],
        compiler_params=params(),
        cost_estimate=pl.CostEstimate(flops=10**9, bytes_accessed=10**6, transcendentals=0),
        name="cross_part",
    )(near_rows, far_rows, before, x1, z1, single, diagonal)


def mid_kernel(own, near_rows, far_rows, first, swapped, partial, cross):
    fill_cross(lambda u, t: swapped[cross_start(u) + 10 - t - u], cross)
    for c in range(NCOL // 2):
        at = cut(2 * c, 2)
        value = nn(own[...], near_rows[:, at])
        if c < 5:
            width = (10 - 2 * c) * BS
            value += first[:, at]
            value += nn(far_rows[:, :width], cross[:width, at])
        partial[:, at] = value


def mid_part(own, near_rows, far_rows, first, swapped):
    return pl.pallas_call(
        mid_kernel,
        out_shape=jax.ShapeDtypeStruct(near_rows.shape, jnp.float32),
        in_specs=[VM] * 5,
        out_specs=VM,
        scratch_shapes=[pltpu.VMEM((10 * BS, 10 * BS), near_rows.dtype)],
        compiler_params=params(),
        cost_estimate=pl.CostEstimate(flops=2 * 10**9, bytes_accessed=10**6, transcendentals=0),
        name="mid_part",
    )(own, near_rows, far_rows, first, swapped)


LOW, LAST = 5, 9


def fill_near(facing, x1, x2, z1, z2, g, h, single, pairs1, pairs2, pairs3):
    def block(t, s):
        if t == NEAR:
            return jnp.where(facing, h[14], single[0])
        if t >= LAST:
            at = near_start(t) + s - t
            return jnp.where(facing, h[at], g[at])
        if t >= LOW:
            start = 14 + sum(13 - n for n in range(t - LOW))
            return jnp.where(facing, z1[start + s - t], z2[near_start(t) + s - t])
        if t == 4 and LOW <= s < LOW + MOVED:
            at = s - LOW
            return turned(jnp.where(facing, z1[60 + at], z2[30 + at]))
        slots = low_slots(t - 1)
        at = sum(len(low_slots(n)) for n in range(t - 1)) + slots.index(HALF + s - t)
        return jnp.where(facing, x1[30 + at], x2[at])

    fill_pairs(block, range(1, LOW), 1, pairs1)
    fill_pairs(block, range(LOW, LAST), LOW, pairs2)
    fill_pairs(block, range(LAST, NEAR + 1), LAST, pairs3)
    pairs3[cut(NCOL - LAST), :] = jnp.zeros((BS, (NCOL + 1 - LAST) * BS), pairs3.dtype)


def near_products(half, near_rows, partial, pairs1, pairs2, pairs3):
    rows = slice(2 * half * BS, (2 * half + 2) * BS)
    two, three = (LOW - 1) * BS, (LAST - 1) * BS
    for c in range(NCOL // 2):
        at = 2 * c * BS
        to = at + 2 * BS
        value = partial[rows, at:to]
        if at < two:
            value += nt(near_rows[rows, :], pairs1[at:to, :])
        else:
            value += nn(near_rows[rows, :two], pairs1[:, at:to])
        if two <= at < three:
            value += nt(near_rows[rows, two:], pairs2[at - two : to - two, :])
        elif at >= three:
            value += nn(near_rows[rows, two:three], pairs2[:, at - two : to - two])
            value += nt(near_rows[rows, three:], pairs3[at - three : to - three, :])
        for n in range(2):
            t = 2 * c + 1 + n
            for e in range(2):
                if 2 * half + e + t <= HALF:
                    yield e, t, value[cut(e), cut(n)]


def away_kernel(near_rows, partial, x1, x2, z1, z2, g, h, single, away, pairs1, pairs2, pairs3):
    fill_near(faces_pair(), x1, x2, z1, z2, g, h, single, pairs1, pairs2, pairs3)
    for e, t, value in near_products(1, near_rows, partial, pairs1, pairs2, pairs3):
        away[e * 11 + t - 1] = value.astype(away.dtype)


def away_part(near_rows, partial, x1, x2, z1, z2, g, h, single):
    shapes = (21, BS, BS), (4 * BS, NEAR_W), (4 * BS, 10 * BS), (6 * BS, 6 * BS)
    return pl.pallas_call(
        away_kernel,
        out_shape=[jax.ShapeDtypeStruct(shape, x1.dtype) for shape in shapes],
        in_specs=[VM] * 9,
        out_specs=[VM] * 4,
        compiler_params=params(),
        cost_estimate=pl.CostEstimate(flops=2 * 10**9, bytes_accessed=10**6, transcendentals=0),
        name="away_part",
    )(near_rows, partial, x1, x2, z1, z2, g, h, single)


def near_kernel(mask, near_rows, partial, inner, pairs1, pairs2, pairs3, out, held, sems):
    core = my_core()
    copies = []

    def put(e, w, value):
        r = jnp.where(core > 0, 1 - e, e)
        a = jnp.where(core > 0, BAND - 1 - w, w)
        held[r, a] = jnp.where(mask[r, a] > 0, value, 0.0).astype(held.dtype)

    def send(e, lo, n):
        r = jnp.where(core > 0, 1 - e, e)
        part = pl.ds(jnp.where(core > 0, BAND - lo - n, lo), n)
        copy = pltpu.make_async_copy(held.at[r, part], out.at[r, part], sems.at[len(copies)])
        copy.start()
        copies.append(copy)

    for e in range(2):
        for k in range(4):
            put(e, k - e + HALF, inner[cut(e), cut(k)])
        send(e, HALF - e, 4)
    for e, t, value in near_products(0, near_rows, partial, pairs1, pairs2, pairs3):
        put(e, HALF - e - t, value)
        if t % 2 == 0:
            send(e, HALF - e - t, 2)
        elif e + t == HALF:
            send(e, 0, 1)
    for copy in copies:
        copy.wait()


def near_part(mask, near_rows, partial, inner, *pairs):
    return pl.pallas_call(
        near_kernel,
        out_shape=jax.ShapeDtypeStruct((2, BAND, BS, BS), near_rows.dtype),
        in_specs=[VM] * 7,
        out_specs=HB,
        scratch_shapes=[
            pltpu.VMEM((2, BAND, BS, BS), near_rows.dtype),
            pltpu.SemaphoreType.DMA((16,)),
        ],
        compiler_params=params(),
        cost_estimate=pl.CostEstimate(flops=10**9, bytes_accessed=10**6, transcendentals=0),
        name="near_part",
    )(mask, near_rows, partial, inner, *pairs)


def join_kernel(mask, came, _, out, held, sems):
    core = my_core()
    copies = []
    for e, count, base in ((0, 10, 11), (1, 11, 0)):
        r = jnp.where(core > 0, 1 - e, e)

        @pl.loop(0, count)
        def _(n):
            w = BAND - count + n
            a = jnp.where(core > 0, BAND - 1 - w, w)
            spot = jnp.where(core > 0, count - 1 - n, n)
            x = came[base + n]
            held[base + spot] = jnp.where(mask[r, a] > 0, x, jnp.zeros_like(x))

        start = jnp.where(core > 0, 0, BAND - count)
        copy = pltpu.make_async_copy(
            held.at[pl.ds(base, count)], out.at[r, pl.ds(start, count)], sems.at[e]
        )
        copy.start()
        copies.append(copy)
    for copy in copies:
        copy.wait()


def join(mask, came, out):
    anywhere = pl.BlockSpec(memory_space=pl.ANY)
    return pl.pallas_call(
        join_kernel,
        out_shape=jax.ShapeDtypeStruct(out.shape, out.dtype),
        in_specs=[VM, VM, anywhere],
        out_specs=anywhere,
        scratch_shapes=[
            pltpu.VMEM(came.shape, came.dtype),
            pltpu.SemaphoreType.DMA((2,)),
        ],
        input_output_aliases={2: 0},
        compiler_params=params(),
        name="join",
    )(mask, came, out)


def body(blocks, columns, counts):
    table = jnp.pad(columns, ((0, 1), (0, 0))) + jnp.pad(counts[None], ((2, 0), (0, BAND - 2)))
    mine, other, mask = own_rows(table, blocks)
    part = to_partner(other)

    def outer(i):
        return not inner(i)

    x1, z1, z2, corner, diagonal = first_packs(mine, part)

    def along(pair, senders):
        def target(i):
            chip, core = divmod(i, 2)
            return 2 * (chip + (pair if core else -pair)) + core if senders(i) else -1

        return target

    x1 = to_side(x1, 1, inner)
    z1 = permute(z1, along(-2, inner))
    corner = permute(corner, along(-3, outer))
    diagonal = permute(diagonal, along(-4, outer))
    own, inside, near_rows, far_rows, sums = own_part(mine, part)

    x2, g, h = second_packs(x1, z1, sums, sums)
    swapped = permute(join_cross(x1, z1, corner, g), lambda i: i ^ 1 if inner(i) else -1)

    z2 = to_side(z2, 2, inner)
    x2 = permute(x2, along(1, inner))
    g = permute(g, along(-1, inner))
    h = permute(h, along(-2, inner))

    first, sums = cross_part(near_rows, far_rows, sums, x1, z1, corner, diagonal)
    sums, swapped = lax.optimization_barrier((sums[:, 0], swapped))
    steps = [1 << n for n in range(lax.axis_size(AXES).bit_length() - 1)]
    sums = sum_over(sums, steps[4:] + steps[:1] + steps[1:2] + steps[3:4])
    partial = mid_part(own, near_rows, far_rows, first, swapped)
    partial, sums = lax.optimization_barrier((partial, sums))
    away, *pairs = away_part(near_rows, partial, x1, x2, z1, z2, g, h, diagonal)
    came = to_partner(away)
    out = near_part(mask, near_rows, partial, inside, *pairs)
    traces = sum_over(sums, steps[2:3])
    square = join(mask, came, out)
    return square, traces


def solution(mesh):
    return jax.shard_map(
        body,
        mesh=mesh,
        in_specs=(P(AXES, None, None, None), P(AXES, None), P(AXES)),
        out_specs=(P(AXES, None, None, None), P()),
        check_vma=False,
    )
```

```python
import jax
import jax.numpy as jnp
from jax import lax
from jax.experimental import pallas as pl
from jax.experimental.pallas import tpu as pltpu
from jax.sharding import PartitionSpec as P

AXES = ("row", "col")
HALF = 13
BAND = 2 * HALF + 1
BS = 128
NEAR = HALF
MOVED = (3, 1)
FAR = 12
NCOL = NEAR + 1
NEAR_W, OWN_W, FAR_W = NCOL * BS, 4 * BS, FAR * BS
OWN_AT, FAR_AT = NEAR_W, NEAR_W + OWN_W
VMEM_LIMIT = 20 * 1024 * 1024

VM = pl.BlockSpec(memory_space=pltpu.VMEM)
SM = pl.BlockSpec(memory_space=pltpu.SMEM)
HB = pl.BlockSpec(memory_space=pl.ANY)


def params():
    return pltpu.CompilerParams(vmem_limit_bytes=VMEM_LIMIT)


def permute(value, target):
    devices = lax.axis_size(AXES)
    pairs = [(i, target(i)) for i in range(devices)]
    return lax.ppermute(value, AXES, [(i, j) for i, j in pairs if 0 <= j < devices])


def to_partner(value):
    return permute(value, lambda i: i ^ 1)


def to_side(value, distance, senders=lambda i: True):
    def target(i):
        chip, core = divmod(i, 2)
        if not senders(i):
            return -1
        return 2 * (chip + distance) if core else 2 * (chip - distance) + 1

    return permute(value, target)


def inner(i):
    return (i // 2 + i % 2) % 2 == 1


def sum_over(value, steps):
    for step in steps:
        value = value + permute(value, lambda i: i ^ step)
    return value


def nn(a, b):
    return lax.dot_general(a, b, (((1,), (0,)), ((), ())), preferred_element_type=jnp.float32)


def nt(a, b):
    return lax.dot_general(a, b, (((1,), (1,)), ((), ())), preferred_element_type=jnp.float32)


def cut(i, n=1):
    return slice(i * BS, (i + n) * BS)


def my_core():
    return lax.rem(lax.axis_index("col"), 2)


def faces_pair():
    index = lax.axis_index("row") * lax.axis_size("col") + lax.axis_index("col")
    return lax.rem(lax.div(index, 2) + lax.rem(index, 2), 2) > 0


def own_kernel(table, blocks, mine, other, mask, flags):
    core = my_core()
    first_row = 2 * (lax.axis_index("row") * lax.axis_size("col") + lax.axis_index("col"))
    for r in range(2):
        for w in range(BAND):
            flags[r, w] = 0
    for r in range(2):

        @pl.loop(0, table[2, r])
        def _(n):
            flags[r, table[r, n] - first_row - r + HALF] = 1

    for r in range(2):
        e = jnp.where(core > 0, 1 - r, r)
        for a in range(BAND):
            keep = flags[r, a]
            mask[r, a] = jnp.full((1, BS), keep, jnp.int32)
            x = jnp.where(keep > 0, blocks[r, a], jnp.zeros((BS, BS), blocks.dtype))
            w = jnp.where(core > 0, BAND - 1 - a, a)
            mine[e, w] = x
            other[1 - e, BAND - 1 - w] = x


def own_rows(table, blocks):
    shape = jax.ShapeDtypeStruct(blocks.shape, blocks.dtype)
    return pl.pallas_call(
        own_kernel,
        out_shape=(shape, shape, jax.ShapeDtypeStruct((2, BAND, 1, BS), jnp.int32)),
        in_specs=[SM, VM],
        out_specs=(VM, VM, VM),
        scratch_shapes=[pltpu.SMEM((2, BAND), jnp.int32)],
        compiler_params=params(),
        name="own_rows",
    )(table, blocks)


def low_slots(e, moved):
    return [w for w in range(HALF, BAND - 1 - e) if e < 3 or not 5 <= w - HALF + 1 + e < 5 + moved]


def first_kernel(mine, part, x1, z1, z2, corner, diagonal):
    at = {}

    def put(out, e, slots):
        for w in slots:
            n = at.get(id(out), 0)
            out[n] = mine[e, w] if e < 2 else part[e - 2, w]
            at[id(out)] = n + 1

    for e in range(4):
        put(x1, e, range(9 - e))
    for e in range(4):
        put(z1, 3 - e, range(BAND - 1, BAND - 6 + e, -1))
    for e in range(4):
        put(z2, e, range(HALF, BAND - 5 - e))
    for e in range(4):
        put(x1, e, low_slots(e, MOVED[0]))
    for e in range(4):
        put(z1, 3 - e, range(HALF, e, -1))
    for e in range(MOVED[0]):
        put(z1, 3 - e, [HALF + 1 + e])
    for e in range(MOVED[1]):
        put(z2, e, [HALF - 1 - e])
    corner[0] = part[1, BAND - 1]
    diagonal[0] = part[1, HALF]


def first_packs(mine, part):
    sizes = (76 - MOVED[0], 60 + MOVED[0], 30 + MOVED[1], 1, 1)
    return pl.pallas_call(
        first_kernel,
        out_shape=[jax.ShapeDtypeStruct((n, BS, BS), mine.dtype) for n in sizes],
        in_specs=[VM] * 2,
        out_specs=[VM] * 5,
        compiler_params=params(),
        name="first_packs",
    )(mine, part)


def second_kernel(x1, z1, _sums, _diagonal, x2, g, h):
    at1 = at2 = 0
    start_x, start_z = 30, 14
    for e in range(4):
        for w in low_slots(e, MOVED[1]):
            x2[at1] = z1[start_z + w - HALF]
            at1 += 1
        for n in range(5 - e):
            g[at2] = z1[start_z + n]
            h[at2] = x1[start_x + n] if n < 4 - e or e < 3 or not MOVED[0] else turned(z1[60])
            at2 += 1
        start_x += len(low_slots(e, MOVED[0]))
        start_z += 13 - e
    h[at2] = z1[14]


def second_packs(x1, z1, sums, diagonal):
    return pl.pallas_call(
        second_kernel,
        out_shape=[jax.ShapeDtypeStruct((n, BS, BS), x1.dtype) for n in (46 - MOVED[1], 14, 15)],
        in_specs=[VM] * 4,
        out_specs=[VM] * 3,
        compiler_params=params(),
        name="second_packs",
    )(x1, z1, sums, diagonal)


def join_cross_kernel(x1, z1, single, _, cross):
    for n in range(30):
        cross[n] = x1[n]
    for n in range(14):
        cross[30 + n] = z1[n]
    cross[44] = single[0]


def join_cross(x1, z1, single, sums):
    return pl.pallas_call(
        join_cross_kernel,
        out_shape=jax.ShapeDtypeStruct((45, BS, BS), x1.dtype),
        in_specs=[VM] * 4,
        out_specs=VM,
        compiler_params=params(),
        name="join_cross",
    )(x1, z1, single, sums)


def turned(x):
    return jnp.transpose(x.astype(jnp.float32)).astype(x.dtype)


def fill_rows(mine, part, rows):
    zero = jnp.zeros((BS, BS), rows.dtype)

    def block(e, k):
        w = k - e + HALF
        if not 0 <= w < BAND:
            return zero
        return mine[e, w] if e < 2 else part[e - 2, w]

    for e in range(4):
        for t in range(1, NCOL + 1):
            rows[cut(e), cut(t - 1)] = block(e, -t)
        for k in range(4):
            rows[cut(e), OWN_AT + k * BS : OWN_AT + (k + 1) * BS] = block(e, k)
        for u in range(1, FAR + 1):
            rows[cut(e), FAR_AT + (u - 1) * BS : FAR_AT + u * BS] = block(e, 3 + u)


def fill_pairs(block, near, low, pairs):
    for t in near:
        for s in range(low, NCOL + 1):
            if s > NEAR:
                x = jnp.zeros((BS, BS), pairs.dtype)
            else:
                x = turned(block(s, t)) if s < t else block(t, s)
            pairs[cut(t - low), cut(s - low)] = x


def near_start(t):
    first = 4 * ((t - 1) // 4) + 1
    return sum(14 - s for s in range(first, t))


def cross_start(t):
    return sum(10 - s for s in range(1, t))


def own_kernel_products(mine, part, own_rows, inner, near_rows, far_rows, sums, rows):
    fill_rows(mine, part, rows)
    own_rows[...] = rows[:, OWN_AT:FAR_AT]
    near_rows[...] = rows[:, :NEAR_W]
    far_rows[...] = rows[:, FAR_AT : FAR_AT + 10 * BS]
    own = rows[:, OWN_AT:FAR_AT]
    third = jnp.zeros((1, 1), jnp.float32)
    for c in range(NCOL // 2):
        near = rows[:, cut(2 * c, 2)]
        value = nn(own, near)
        third += jnp.sum(near.astype(jnp.float32) * value, keepdims=True)
    third = 3.0 * third
    top = rows[: 2 * BS, OWN_AT:FAR_AT]
    third += jnp.sum(top.astype(jnp.float32) * nn(top, own), keepdims=True)
    inner[...] = nt(rows[: 2 * BS, :], rows[...])
    second = jnp.zeros((1, 1), jnp.float32)
    for e in range(2):
        for w in range(BAND):
            x = mine[e, w].astype(jnp.float32)
            second += jnp.sum(x * x, keepdims=True)
    sums[0:1, :] = jnp.broadcast_to(second, (1, BS))
    sums[1:2, :] = jnp.broadcast_to(third, (1, BS))


def own_part(mine, part):
    return pl.pallas_call(
        own_kernel_products,
        out_shape=(
            jax.ShapeDtypeStruct((4 * BS, OWN_W), mine.dtype),
            jax.ShapeDtypeStruct((2 * BS, OWN_W), jnp.float32),
            jax.ShapeDtypeStruct((4 * BS, NEAR_W), mine.dtype),
            jax.ShapeDtypeStruct((4 * BS, 10 * BS), mine.dtype),
            jax.ShapeDtypeStruct((2, BS), jnp.float32),
        ),
        in_specs=[VM] * 2,
        out_specs=(VM,) * 5,
        scratch_shapes=[pltpu.VMEM((4 * BS, FAR_AT + FAR_W), mine.dtype)],
        compiler_params=params(),
        cost_estimate=pl.CostEstimate(flops=2 * 10**9, bytes_accessed=10**6, transcendentals=0),
        name="own_part",
    )(mine, part)


def fill_cross(block, pairs):
    for c in range(5):
        for g in range(5 - c):
            for n in (2 * c + 1, 2 * c + 2):
                for m in (2 * g + 1, 2 * g + 2):
                    x = block(n, m) if n + m <= 10 else jnp.zeros((BS, BS), pairs.dtype)
                    pairs[cut(n - 1), cut(m - 1)] = x


def cross_kernel(near_rows, far_rows, before, x1, z1, single, _diagonal, first, sums, pairs):
    def block(t, u):
        at = cross_start(t) + 10 - t - u
        if t == 9:
            return jnp.where(faces_pair(), single[0], jnp.zeros((BS, BS), pairs.dtype))
        return x1[at] if t < 5 else z1[at - 30]

    fill_cross(block, pairs)
    third = jnp.zeros((1, 1), jnp.float32)
    for c in range(5):
        at = cut(2 * c, 2)
        width = (10 - 2 * c) * BS
        value = nt(far_rows[:, :width], pairs[at, :width])
        first[:, at] = value
        third += jnp.sum(near_rows[:, at].astype(jnp.float32) * value, keepdims=True)
    scale = 1.0 / (2 * BS * lax.axis_size(AXES))
    sums[0:1, :] = before[0:1, :] * scale
    sums[1:2, :] = (before[1:2, :] + 6.0 * third) * scale


def cross_part(near_rows, far_rows, before, x1, z1, single, diagonal):
    return pl.pallas_call(
        cross_kernel,
        out_shape=(
            jax.ShapeDtypeStruct((4 * BS, 10 * BS), jnp.float32),
            jax.ShapeDtypeStruct(before.shape, jnp.float32),
        ),
        in_specs=[VM] * 7,
        out_specs=(VM,) * 2,
        scratch_shapes=[pltpu.VMEM((10 * BS, 10 * BS), x1.dtype)],
        compiler_params=params(),
        cost_estimate=pl.CostEstimate(flops=10**9, bytes_accessed=10**6, transcendentals=0),
        name="cross_part",
    )(near_rows, far_rows, before, x1, z1, single, diagonal)


def mid_kernel(own, near_rows, far_rows, first, swapped, partial, cross):
    fill_cross(lambda u, t: swapped[cross_start(u) + 10 - t - u], cross)
    for c in range(NCOL // 2):
        at = cut(2 * c, 2)
        value = nn(own[...], near_rows[:, at])
        if c < 5:
            width = (10 - 2 * c) * BS
            value += first[:, at]
            value += nn(far_rows[:, :width], cross[:width, at])
        partial[:, at] = value


def mid_part(own, near_rows, far_rows, first, swapped):
    return pl.pallas_call(
        mid_kernel,
        out_shape=jax.ShapeDtypeStruct(near_rows.shape, jnp.float32),
        in_specs=[VM] * 5,
        out_specs=VM,
        scratch_shapes=[pltpu.VMEM((10 * BS, 10 * BS), near_rows.dtype)],
        compiler_params=params(),
        cost_estimate=pl.CostEstimate(flops=2 * 10**9, bytes_accessed=10**6, transcendentals=0),
        name="mid_part",
    )(own, near_rows, far_rows, first, swapped)


LOW, LAST = 5, 9


def fill_near(facing, x1, x2, z1, z2, g, h, single, pairs1, pairs2, pairs3):
    def block(t, s):
        if t == NEAR:
            return jnp.where(facing, h[14], single[0])
        if t >= LAST:
            at = near_start(t) + s - t
            return jnp.where(facing, h[at], g[at])
        if t >= LOW:
            start = 14 + sum(13 - n for n in range(t - LOW))
            return jnp.where(facing, z1[start + s - t], z2[near_start(t) + s - t])
        found = []
        for moved, straight, start, along, more in zip(MOVED, (x1, x2), (30, 0), (z1, z2), (60, 30)):
            if t == 4 and LOW <= s < LOW + moved:
                found.append(turned(along[more + s - LOW]))
            else:
                at = sum(len(low_slots(n, moved)) for n in range(t - 1))
                at += low_slots(t - 1, moved).index(HALF + s - t)
                found.append(straight[start + at])
        return jnp.where(facing, *found)

    fill_pairs(block, range(1, LOW), 1, pairs1)
    fill_pairs(block, range(LOW, LAST), LOW, pairs2)
    fill_pairs(block, range(LAST, NEAR + 1), LAST, pairs3)
    pairs3[cut(NCOL - LAST), :] = jnp.zeros((BS, (NCOL + 1 - LAST) * BS), pairs3.dtype)


def near_products(half, near_rows, partial, pairs1, pairs2, pairs3):
    rows = slice(2 * half * BS, (2 * half + 2) * BS)
    two, three = (LOW - 1) * BS, (LAST - 1) * BS
    for c in range(NCOL // 2):
        at = 2 * c * BS
        to = at + 2 * BS
        value = partial[rows, at:to]
        if at < two:
            value += nt(near_rows[rows, :], pairs1[at:to, :])
        else:
            value += nn(near_rows[rows, :two], pairs1[:, at:to])
        if two <= at < three:
            value += nt(near_rows[rows, two:], pairs2[at - two : to - two, :])
        elif at >= three:
            value += nn(near_rows[rows, two:three], pairs2[:, at - two : to - two])
            value += nt(near_rows[rows, three:], pairs3[at - three : to - three, :])
        for n in range(2):
            t = 2 * c + 1 + n
            for e in range(2):
                if 2 * half + e + t <= HALF:
                    yield e, t, value[cut(e), cut(n)]


def away_kernel(near_rows, partial, x1, x2, z1, z2, g, h, single, away, pairs1, pairs2, pairs3):
    fill_near(faces_pair(), x1, x2, z1, z2, g, h, single, pairs1, pairs2, pairs3)
    for e, t, value in near_products(1, near_rows, partial, pairs1, pairs2, pairs3):
        away[e * 11 + t - 1] = value.astype(away.dtype)


def away_part(near_rows, partial, x1, x2, z1, z2, g, h, single):
    shapes = (21, BS, BS), (4 * BS, NEAR_W), (4 * BS, 10 * BS), (6 * BS, 6 * BS)
    return pl.pallas_call(
        away_kernel,
        out_shape=[jax.ShapeDtypeStruct(shape, x1.dtype) for shape in shapes],
        in_specs=[VM] * 9,
        out_specs=[VM] * 4,
        compiler_params=params(),
        cost_estimate=pl.CostEstimate(flops=2 * 10**9, bytes_accessed=10**6, transcendentals=0),
        name="away_part",
    )(near_rows, partial, x1, x2, z1, z2, g, h, single)


def near_kernel(mask, near_rows, partial, inner, pairs1, pairs2, pairs3, out, held, sems):
    core = my_core()
    copies = []

    def put(e, w, value):
        r = jnp.where(core > 0, 1 - e, e)
        a = jnp.where(core > 0, BAND - 1 - w, w)
        held[r, a] = jnp.where(mask[r, a] > 0, value, 0.0).astype(held.dtype)

    def send(e, lo, n):
        r = jnp.where(core > 0, 1 - e, e)
        part = pl.ds(jnp.where(core > 0, BAND - lo - n, lo), n)
        copy = pltpu.make_async_copy(held.at[r, part], out.at[r, part], sems.at[len(copies)])
        copy.start()
        copies.append(copy)

    for e in range(2):
        for k in range(4):
            put(e, k - e + HALF, inner[cut(e), cut(k)])
        send(e, HALF - e, 4)
    for e, t, value in near_products(0, near_rows, partial, pairs1, pairs2, pairs3):
        put(e, HALF - e - t, value)
        if t % 2 == 0:
            send(e, HALF - e - t, 2)
        elif e + t == HALF:
            send(e, 0, 1)
    for copy in copies:
        copy.wait()


def near_part(mask, near_rows, partial, inner, *pairs):
    return pl.pallas_call(
        near_kernel,
        out_shape=jax.ShapeDtypeStruct((2, BAND, BS, BS), near_rows.dtype),
        in_specs=[VM] * 7,
        out_specs=HB,
        scratch_shapes=[
            pltpu.VMEM((2, BAND, BS, BS), near_rows.dtype),
            pltpu.SemaphoreType.DMA((16,)),
        ],
        compiler_params=params(),
        cost_estimate=pl.CostEstimate(flops=10**9, bytes_accessed=10**6, transcendentals=0),
        name="near_part",
    )(mask, near_rows, partial, inner, *pairs)


def join_kernel(mask, came, _, out, held, sems):
    core = my_core()
    copies = []
    for e, count, base in ((0, 10, 11), (1, 11, 0)):
        r = jnp.where(core > 0, 1 - e, e)

        @pl.loop(0, count)
        def _(n):
            w = BAND - count + n
            a = jnp.where(core > 0, BAND - 1 - w, w)
            spot = jnp.where(core > 0, count - 1 - n, n)
            x = came[base + n]
            held[base + spot] = jnp.where(mask[r, a] > 0, x, jnp.zeros_like(x))

        start = jnp.where(core > 0, 0, BAND - count)
        copy = pltpu.make_async_copy(
            held.at[pl.ds(base, count)], out.at[r, pl.ds(start, count)], sems.at[e]
        )
        copy.start()
        copies.append(copy)
    for copy in copies:
        copy.wait()


def join(mask, came, out):
    anywhere = pl.BlockSpec(memory_space=pl.ANY)
    return pl.pallas_call(
        join_kernel,
        out_shape=jax.ShapeDtypeStruct(out.shape, out.dtype),
        in_specs=[VM, VM, anywhere],
        out_specs=anywhere,
        scratch_shapes=[
            pltpu.VMEM(came.shape, came.dtype),
            pltpu.SemaphoreType.DMA((2,)),
        ],
        input_output_aliases={2: 0},
        compiler_params=params(),
        name="join",
    )(mask, came, out)


def body(blocks, columns, counts):
    table = jnp.pad(columns, ((0, 1), (0, 0))) + jnp.pad(counts[None], ((2, 0), (0, BAND - 2)))
    mine, other, mask = own_rows(table, blocks)
    part = to_partner(other)

    def outer(i):
        return not inner(i)

    x1, z1, z2, corner, diagonal = first_packs(mine, part)

    def along(pair, senders):
        def target(i):
            chip, core = divmod(i, 2)
            return 2 * (chip + (pair if core else -pair)) + core if senders(i) else -1

        return target

    x1 = to_side(x1, 1, inner)
    z1 = permute(z1, along(-2, inner))
    corner = permute(corner, along(-3, outer))
    diagonal = permute(diagonal, along(-4, outer))
    own, inside, near_rows, far_rows, sums = own_part(mine, part)

    x2, g, h = second_packs(x1, z1, sums, sums)
    swapped = permute(join_cross(x1, z1, corner, g), lambda i: i ^ 1 if inner(i) else -1)

    z2 = to_side(z2, 2, inner)
    x2 = permute(x2, along(1, inner))
    g = permute(g, along(-1, inner))
    h = permute(h, along(-2, inner))

    first, sums = cross_part(near_rows, far_rows, sums, x1, z1, corner, diagonal)
    sums, swapped = lax.optimization_barrier((sums[:, 0], swapped))
    steps = [1 << n for n in range(lax.axis_size(AXES).bit_length() - 1)]
    sums = sum_over(sums, steps[4:] + steps[:1] + steps[1:3])
    partial = mid_part(own, near_rows, far_rows, first, swapped)
    partial, sums = lax.optimization_barrier((partial, sums))
    away, *pairs = away_part(near_rows, partial, x1, x2, z1, z2, g, h, diagonal)
    came = to_partner(away)
    out = near_part(mask, near_rows, partial, inside, *pairs)
    traces = sum_over(sums, steps[3:4])
    square = join(mask, came, out)
    return square, traces


def solution(mesh):
    return jax.shard_map(
        body,
        mesh=mesh,
        in_specs=(P(AXES, None, None, None), P(AXES, None), P(AXES)),
        out_specs=(P(AXES, None, None, None), P()),
        check_vma=False,
    )
```
